512 devices in a mesh: ctx: 64 (over z_lo, y, core), tp: 8 (over x, z_hi).
Axes of the slice: x: 4, y: 4, z: 16 (z_hi: 2, z_lo: 8; z = z_hi * 8 + z_lo), core: 2. Of those that a mesh axis runs over, the one named last changes fastest.
Arguments:
- projected: bfloat16 [3, 16384, 2048], P(None, 'ctx', 'tp'), may hold values from -6 to 6
- short_filter: float32 [3, 3, 2048], P(None, None, 'tp'), may hold values from -4 to 4
- decay_rates: float32 [16, 2048], P(None, 'tp'), may hold values from 6.1035156e-05 to 0.05
- residues: float32 [16, 2048], P(None, 'tp'), may hold values from -0.09375 to 0.09375
- output_grad: bfloat16 [16384, 2048], P('ctx', 'tp'), may hold values from -6 to 6
- clip_bound: float32 [1], replicated, may hold values from 2085.3428 to 8688928
Outputs:
- gated_output: bfloat16 [16384, 2048], P('ctx', 'tp')
- projected_grads: bfloat16 [3, 16384, 2048], P(None, 'ctx', 'tp')
- filter_grads: float32 [3, 3, 2048], P(None, None, 'tp')
The draws below stay inside these ranges and needn't reach their ends.
All inputs are finite; a program needn't handle non-finite values.
Results may differ from the reference program's by a relative error of at most 0.0082.
Values may be sent and summed in bfloat16 or wider, within the bound.
A program may use at most 64 MiB of HBM per device.

```python
import math
import jax
import jax.numpy as jnp
from jax import lax

C = 2048
TAPS = 3
ORDER = 16
FB = 512
SEQ = 16384


def draw_clip_bound(key, part):
    key = jax.random.fold_in(key, 7)
    uniform_part = jax.random.uniform(key, (1,), jnp.float32)
    norm_scale = (3.0 * TAPS * C * SEQ) ** 0.5
    drawn = norm_scale * (0.12 + 0.13 * uniform_part)
    return drawn.astype(jnp.float32)


def shard_levels(key, dims, shards, low, largest):
    factor_of, own = 1.0, jax.random.fold_in(key, 6)
    for dim, shards_of in shards:
        steps = jnp.exp(jax.random.uniform(jax.random.fold_in(own, dim), (shards_of,), jnp.float32, low / len(shards), largest / len(shards)))
        factor_of = factor_of * jnp.repeat(steps, dims[dim] // shards_of).reshape([-1 if axis == dim else 1 for axis in range(len(dims))])
    return factor_of


def noise(key, shape, deviation, reach, split=(), kind=jnp.bfloat16):
    result = jax.random.normal(key, shape, jnp.float32) * deviation
    if len(split) > 0:
        result = shard_levels(key, shape, split, -0.22, 0.18) * result
    return jnp.clip(result, min=-reach, max=reach).astype(kind)


def setup_inputs(seed: int = 0) -> dict:
    streams_of = jax.random.split(jax.random.key(seed), 7)
    projected = noise(streams_of[0], (3, SEQ, C), 1.0, 6.0, ((1, 64), (2, 8)))
    short_filter = noise(streams_of[1], (3, TAPS, C), 0.6, 4.0, ((2, 8),), jnp.float32)
    decay_rates = jnp.clip(jnp.exp(math.log(0.05) - 6.7083283 * jax.random.uniform(streams_of[2], (ORDER, C), jnp.float32) ** shard_levels(streams_of[2], (ORDER, C), ((1, 8),), -0.2, 0.2)), 6.103515625e-05, 0.05)
    residues = noise(streams_of[3], (ORDER, C), (3 * (ORDER * SEQ) ** -0.5), 0.09375, ((1, 8),), jnp.float32)
    output_grad = noise(streams_of[4], (SEQ, C), 1.0, 6.0, ((0, 64), (1, 8)))
    clip_bound = draw_clip_bound(jax.random.fold_in(streams_of[6], 71), 0)
    return {"projected": projected, "short_filter": short_filter, "decay_rates": decay_rates, "residues": residues, "output_grad": output_grad, "clip_bound": clip_bound}


def trig_table(rows, cols, modulus):
    index = jnp.arange(rows, dtype=jnp.int32)[:, None] * jnp.arange(cols, dtype=jnp.int32)[None, :] % modulus
    angle = index.astype(jnp.float32) * (2.0 * math.pi / modulus)
    return (jnp.cos(angle), jnp.sin(angle))

def filter_spectrum(rates, weights, freq_rows, cols):
    total = freq_rows * cols
    low = jnp.arange(freq_rows, dtype=jnp.int32)[:, None]
    high = jnp.arange(cols, dtype=jnp.int32)[None, :]
    index = low + freq_rows * high
    half_angle = index.astype(jnp.float32) * (math.pi / total)
    sine_half = jnp.sin(half_angle)[:, None, :]
    sine_full = jnp.sin(2.0 * half_angle)[:, None, :]
    parity = (1 - 2 * (index % 2)).astype(jnp.float32)[:, None, :]
    bend = 2.0 * sine_half * sine_half
    resp_real = jnp.zeros((freq_rows, rates.shape[1], cols), jnp.float32)
    resp_imag = jnp.zeros((freq_rows, rates.shape[1], cols), jnp.float32)
    for mode in range(rates.shape[0]):
        rate = rates[mode][None, :, None]
        keep = jnp.exp(-rate)
        gap = -jnp.expm1(-rate)
        tail = jnp.exp(-rate * (total // 2))
        numer = weights[mode][None, :, None] * (1.0 - tail * parity)
        denom = gap * gap + 2.0 * keep * bend
        resp_real = resp_real + numer * (gap + keep * bend) / denom
        resp_imag = resp_imag - numer * keep * sine_full / denom
    return (resp_real, resp_imag)

def batch_product(form, left, right):
    return jnp.einsum(form, left.astype(jnp.float32), right.astype(jnp.float32), precision=lax.Precision.HIGHEST)

def filter_pass(real_in, imag_in, resp_real, resp_imag):
    rows = real_in.shape[0]
    freq_rows = 2 * rows
    channels = real_in.shape[1] // FB
    total = freq_rows * FB
    cos_a, sin_a = trig_table(freq_rows, rows, freq_rows)
    table_a = jnp.concatenate([cos_a, sin_a], axis=0).astype(jnp.bfloat16)
    from_real = jnp.dot(table_a, real_in, preferred_element_type=jnp.float32)
    from_imag = jnp.dot(table_a, imag_in, preferred_element_type=jnp.float32)
    first_real = (from_real[:freq_rows] + from_imag[freq_rows:]).reshape(freq_rows, FB, channels)
    first_imag = (from_imag[:freq_rows] - from_real[freq_rows:]).reshape(freq_rows, FB, channels)
    cos_t, sin_t = trig_table(freq_rows, FB, total)
    cos_t = cos_t[:, :, None]
    sin_t = sin_t[:, :, None]
    twist_real = (first_real * cos_t + first_imag * sin_t).astype(jnp.bfloat16)
    twist_imag = (first_imag * cos_t - first_real * sin_t).astype(jnp.bfloat16)
    cos_b, sin_b = trig_table(FB, FB, FB)
    table_b = jnp.concatenate([cos_b, sin_b], axis=1).astype(jnp.bfloat16)
    second_real = batch_product('kbc,bm->kcm', twist_real, table_b)
    second_imag = batch_product('kbc,bm->kcm', twist_imag, table_b)
    spec_real = second_real[:, :, :FB] + second_imag[:, :, FB:]
    spec_imag = second_imag[:, :, :FB] - second_real[:, :, FB:]
    scale = 1.0 / total
    prod_real = ((resp_real * spec_real - resp_imag * spec_imag) * scale).astype(jnp.bfloat16)
    prod_imag = ((resp_real * spec_imag + resp_imag * spec_real) * scale).astype(jnp.bfloat16)
    back_real = batch_product('kcm,mb->kbc', prod_real, table_b)
    back_imag = batch_product('kcm,mb->kbc', prod_imag, table_b)
    third_real = back_real[:, :FB] - back_imag[:, FB:]
    third_imag = back_imag[:, :FB] + back_real[:, FB:]
    turn_real = (third_real * cos_t - third_imag * sin_t).astype(jnp.bfloat16).reshape(freq_rows, FB * channels)
    turn_imag = (third_imag * cos_t + third_real * sin_t).astype(jnp.bfloat16).reshape(freq_rows, FB * channels)
    cos_c, sin_c = trig_table(rows, freq_rows, freq_rows)
    table_c = jnp.concatenate([cos_c, sin_c], axis=0).astype(jnp.bfloat16)
    last_real = jnp.dot(table_c, turn_real, preferred_element_type=jnp.float32)
    last_imag = jnp.dot(table_c, turn_imag, preferred_element_type=jnp.float32)
    return (last_real[:rows] - last_imag[rows:], last_imag[:rows] + last_real[rows:])

def reference(projected, short_filter, decay_rates, residues, output_grad, clip_bound):
    block_width = min(64, C)
    block_count = C // block_width
    lead = TAPS - 1

    def one_block(index):
        start = index * block_width
        inputs = lax.dynamic_slice_in_dim(projected, start, block_width, 2).astype(jnp.float32)
        weights = lax.dynamic_slice_in_dim(short_filter, start, block_width, 2)
        rates = lax.dynamic_slice_in_dim(decay_rates, start, block_width, 1)
        modes = lax.dynamic_slice_in_dim(residues, start, block_width, 1)
        cotangent = lax.dynamic_slice_in_dim(output_grad, start, block_width, 1).astype(jnp.float32)
        extended = jnp.pad(inputs, ((0, 0), (lead, 0), (0, 0)))
        features = jnp.zeros_like(inputs)
        for j in range(TAPS):
            features = features + weights[:, j][:, None, :] * extended[:, lead - j:lead - j + SEQ]
        mixer_input = (features[1] * features[2]).astype(jnp.bfloat16)
        grad_input = (cotangent * features[0]).astype(jnp.bfloat16)
        rows = SEQ // FB
        real_in = mixer_input.reshape(rows, FB * block_width)
        imag_in = jnp.flip(grad_input, 0).reshape(rows, FB * block_width)
        resp_real, resp_imag = filter_spectrum(rates, modes, 2 * rows, FB)
        out_real, out_imag = filter_pass(real_in, imag_in, resp_real, resp_imag)
        conv_output = out_real.reshape(SEQ, block_width).astype(jnp.bfloat16).astype(jnp.float32)
        conv_grad = jnp.flip(out_imag.reshape(SEQ, block_width), 0).astype(jnp.bfloat16).astype(jnp.float32)
        gated = (features[0] * conv_output).astype(jnp.bfloat16)
        feature_grads = jnp.stack([cotangent * conv_output, conv_grad * features[2], conv_grad * features[1]])
        padded_grads = jnp.pad(feature_grads, ((0, 0), (0, lead), (0, 0)))
        back = jnp.zeros_like(feature_grads)
        sums = []
        for j in range(TAPS):
            back = back + weights[:, j][:, None, :] * padded_grads[:, j:j + SEQ]
            sums.append(lax.optimization_barrier(jnp.sum(feature_grads * extended[:, lead - j:lead - j + SEQ], axis=1)))
        return (gated, back.astype(jnp.bfloat16), jnp.stack(sums, axis=1))
    gated_b, back_b, sums_b = lax.map(one_block, jnp.arange(block_count, dtype=jnp.int32))
    gated_output = jnp.transpose(gated_b, (1, 0, 2)).reshape(SEQ, C)
    projected_grads = jnp.transpose(back_b, (1, 2, 0, 3)).reshape(3, SEQ, C)
    filter_sums = jnp.transpose(sums_b, (1, 2, 0, 3)).reshape(3, TAPS, C)
    grad_norm = jnp.sqrt(jnp.sum(filter_sums * filter_sums))
    bound = clip_bound[0]
    filter_grads = filter_sums * (bound / jnp.maximum(grad_norm, bound))
    return (gated_output, projected_grads, filter_grads)
```

```python
import functools

import jax
import jax.numpy as jnp
from jax import lax
from jax.experimental import pallas as pl
from jax.experimental.pallas import tpu as pltpu
from jax.sharding import PartitionSpec as P

MESH = pl.DeviceIdType.MESH
F32 = jnp.float32
LANES = 128
SUB = 8
PAD = 8
G = 8
HALO, S_GROUP, S_LINE, S_BACK, R_GROUP, R_LINE, R_BACK, NORM, TAIL = range(9)


def kernel(
    modes, tp_size,
    proj, taps, rates, weights, cot, bound,
    gated, grads, filt,
    pf, feat, xs, ys, lam, htab, excl, rown, gat, fgs,
    halo_out, halo_in, tail_out, tail_in,
    sa_out, sa_in, sb_out, sb_in, sc_out, sc_in,
    r1_out, r1_in, r2_out, r2_in, r3_out, r3_in, r4_out, r4_in,
    ssem, rsem,
):
    tokens = proj.shape[1]
    halves = proj.shape[2] // LANES
    block = tokens // SUB
    quarter = modes // (G // 2)
    ctx, tp = lax.axis_index("ctx"), lax.axis_index("tp")
    count = lax.axis_size("ctx")
    lines = count // G
    z, g = ctx // G, lax.rem(ctx, G)
    causal = g < G // 2
    zz = jnp.where(causal, z, lines - 1 - z)
    towards = jnp.where(causal, 1, -1)

    def at_group(d):
        return {"ctx": z * G + lax.rem(g + d, G), "tp": tp}

    def at_line(d):
        return {"ctx": lax.rem(z + d, lines) * G + g, "tp": tp}

    def at_tp(d):
        return {"ctx": ctx, "tp": lax.rem(tp + d, tp_size)}

    def at(c):
        return {"ctx": c, "tp": tp}

    halo_in[...] = jnp.zeros_like(halo_in)
    tail_in[...] = jnp.zeros_like(tail_in)
    sb_in[...] = jnp.zeros_like(sb_in)

    barrier = pltpu.get_barrier_semaphore()
    for d in range(1, G):
        pl.semaphore_signal(barrier, inc=1, device_id=at_group(d), device_id_type=MESH)
    for d in range(1, lines):
        pl.semaphore_signal(barrier, inc=1, device_id=at_line(d), device_id_type=MESH)
    for d in range(1, tp_size):
        pl.semaphore_signal(barrier, inc=1, device_id=at_tp(d), device_id_type=MESH)
    more_next = jnp.logical_and(g == G - 1, ctx < count - 1)
    more_prev = jnp.logical_and(g == 0, ctx > 0)

    @pl.when(more_next)
    def _():
        pl.semaphore_signal(barrier, inc=1, device_id=at(ctx + 1), device_id_type=MESH)

    @pl.when(more_prev)
    def _():
        pl.semaphore_signal(barrier, inc=1, device_id=at(ctx - 1), device_id_type=MESH)

    def send(src, dst, step, d, dev):
        return pltpu.make_async_remote_copy(
            src_ref=src, dst_ref=dst, send_sem=ssem.at[step, d], recv_sem=rsem.at[step, d],
            device_id=dev, device_id_type=MESH,
        )

    halo_out[...] = jnp.zeros_like(halo_out)
    tail_out[...] = jnp.zeros_like(tail_out)
    r1_out[...] = jnp.zeros_like(r1_out)
    for s in range(3):
        last = proj[s, tokens - 16 : tokens, :].astype(F32)
        halo_out[2 * s : 2 * s + 2, :] = last[14:16, :]

    pl.semaphore_wait(
        barrier,
        (G - 1) + (lines - 1) + (tp_size - 1) + jnp.where(more_next, 1, 0) + jnp.where(more_prev, 1, 0),
    )
    halo = send(halo_out, halo_in, HALO, 0, at(ctx + 1))

    @pl.when(ctx < count - 1)
    def _():
        halo.start()

    for h in range(halves):
        cols = slice(h * LANES, (h + 1) * LANES)
        for s in range(3):
            pf[s * halves + h, PAD : PAD + tokens, :] = proj[s, :, cols].astype(F32)
        pf[3 * halves + h, PAD : PAD + tokens, :] = cot[:, cols].astype(F32)

    for m in range(modes):
        rate = rates[m : m + 1, :]
        keep = jnp.exp(-rate)
        for h in range(halves):
            lam[h, m] = jnp.broadcast_to(keep[:, h * LANES : (h + 1) * LANES], (SUB, LANES))
            rown[m // quarter, h * quarter + m % quarter : h * quarter + m % quarter + 1, :] = rate[
                :, h * LANES : (h + 1) * LANES
            ]
    steps = lax.broadcasted_iota(jnp.int32, (block, LANES), 0).astype(F32)
    for h in range(halves):
        cols = slice(h * LANES, (h + 1) * LANES)
        total = jnp.zeros((block, LANES), F32)
        for m in range(modes):
            total = total + weights[m : m + 1, cols] * jnp.exp(-rates[m : m + 1, cols] * steps)
        for k in range(block):
            htab[h, k] = jnp.broadcast_to(total[k : k + 1, :], (SUB, LANES))

    def rows(b):
        return pl.ds(PAD + b, SUB, stride=block)

    def tap(s, j, h):
        return jnp.broadcast_to(taps[s, j : j + 1, h * LANES : (h + 1) * LANES], (SUB, LANES))

    def featurize(b, h):
        f = []
        for s in range(3):
            i = s * halves + h
            value = tap(s, 0, h) * pf[i, rows(b), :]
            value = value + tap(s, 1, h) * pf[i, rows(b - 1), :]
            value = value + tap(s, 2, h) * pf[i, rows(b - 2), :]
            feat[i, b] = value
            f.append(value)
        xs[h, b] = f[1] * f[2]
        xs[halves + h, block - 1 - b] = pf[3 * halves + h, rows(b), :] * f[0]

    for h in range(halves):
        lax.fori_loop(2, block, lambda b, _: featurize(b, h), None)

    @pl.when(ctx > 0)
    def _():
        halo.wait_recv()

    for h in range(halves):
        for s in range(3):
            pf[s * halves + h, PAD - 2 : PAD, :] = halo_in[2 * s : 2 * s + 2, h * LANES : (h + 1) * LANES]
        for b in range(2):
            featurize(b, h)

    place = lax.broadcasted_iota(jnp.int32, (SUB, LANES), 0)
    for h in range(halves):
        cols = slice(h * LANES, (h + 1) * LANES)
        keeps = [lam[h, m] for m in range(modes)]

        def horner(b, state):
            front, back = xs[h, b], xs[halves + h, b]
            return tuple(
                state[2 * m + r] * keeps[m] + (front, back)[r] for m in range(modes) for r in range(2)
            )

        zero = jnp.zeros((SUB, LANES), F32)
        state = lax.fori_loop(0, block, horner, (zero,) * (2 * modes))
        for m in range(modes):
            rate = rates[m : m + 1, cols]
            for r in range(2):
                value = state[2 * m + r]
                for k in (1, 2, 4):
                    fade = jnp.exp(-(block * k) * rate)
                    if r == 0:
                        value = value + jnp.where(place >= k, fade, 0.0) * pltpu.roll(value, k, 0)
                    else:
                        value = value + jnp.where(place < SUB - k, fade, 0.0) * pltpu.roll(value, SUB - k, 0)
                row = h * quarter + m % quarter
                owner = r * (G // 2) + m // quarter
                if r == 0:
                    excl[h, m] = jnp.where(place >= 1, pltpu.roll(value, 1, 0), 0.0)
                    sa_out[owner, row : row + 1, :] = value[SUB - 1 : SUB, :]
                else:
                    excl[halves + h, m] = jnp.where(place < SUB - 1, pltpu.roll(value, SUB - 1, 0), 0.0)
                    sa_out[owner, row : row + 1, :] = value[0:1, :]

    group_out = [send(sa_out.at[lax.rem(g + d, G)], sa_in.at[d], S_GROUP, d, at_group(d)) for d in range(1, G)]
    for copy in group_out:
        copy.start()
    sa_in[0] = sa_out[g]

    def direct(hd, _):
        h = lax.rem(hd, halves)
        width = 8
        for b0 in range(0, block, width):
            acc = [None] * width
            for a0 in range(0, b0 + width, width):
                for a in range(a0, a0 + width):
                    x = xs[hd, a]
                    for i in range(width):
                        if b0 + i >= a:
                            term = htab[h, b0 + i - a] * x
                            acc[i] = term if acc[i] is None else acc[i] + term
            for i in range(width):
                ys[hd, b0 + i] = acc[i]

    lax.fori_loop(0, 2, direct, None)
    for copy in group_out:
        copy.wait_recv()

    own_rate = rown[lax.rem(g, G // 2)]
    fade = jnp.exp(-float(tokens) * own_rate)
    fade_group = jnp.exp(-float(tokens * G) * own_rate)

    def member(i):
        return jnp.where(causal, i, G - 1 - i)

    def slot(i):
        return lax.rem(g - member(i) + G, G)

    value = jnp.zeros((SUB, LANES), F32)
    for i in range(G):
        value = value * fade + sa_in[slot(i)]
    sb_out[...] = value
    line_out = [
        send(sb_out, sb_in.at[d], S_LINE, d, at((z + d * towards) * G + g)) for d in range(1, lines)
    ]
    for d in range(1, lines):
        @pl.when(zz + d < lines)
        def _():
            line_out[d - 1].start()

    lax.fori_loop(2, 3, direct, None)
    for d in range(1, lines):
        @pl.when(zz - d >= 0)
        def _():
            line_out[d - 1].wait_recv()

    value = jnp.zeros((SUB, LANES), F32)
    for d in range(lines - 1, 0, -1):
        value = value * fade_group + sb_in[d]
    for i in range(G):
        sc_out[member(i)] = value
        value = value * fade + sa_in[slot(i)]
    back_out = [send(sc_out.at[lax.rem(g + d, G)], sc_in.at[d], S_BACK, d, at_group(d)) for d in range(1, G)]
    for copy in back_out:
        copy.start()
    sc_in[0] = sc_out[g]
    lax.fori_loop(3, 4, direct, None)
    for copy in back_out:
        copy.wait_recv()

    for h in range(halves):
        cols = slice(h * LANES, (h + 1) * LANES)
        keeps = [lam[h, m] for m in range(modes)]
        for r in range(2):
            ahead = (place if r == 0 else SUB - 1 - place).astype(F32)
            left = []
            for m in range(modes):
                owner = r * (G // 2) + m // quarter
                row = h * quarter + m % quarter
                carry = sc_in[lax.rem(g - owner + G, G), row : row + 1, :]
                rate = rates[m : m + 1, cols]
                value = excl[r * halves + h, m] + jnp.exp(-float(block) * rate * ahead) * carry
                left.append(value * (weights[m : m + 1, cols] * keeps[m]))

            def readout(b, left):
                parts = list(left)
                while len(parts) > 1:
                    parts = [parts[i] + parts[i + 1] for i in range(0, len(parts), 2)]
                ys[r * halves + h, b] = ys[r * halves + h, b] + parts[0]
                return tuple(left[m] * keeps[m] for m in range(modes))

            lax.fori_loop(0, block, readout, tuple(left))

    for h in range(halves):
        def finish(b, sums):
            out, back = ys[h, b], ys[halves + h, block - 1 - b]
            gat[h, pl.ds(b, SUB, stride=block), :] = feat[h, b] * out
            fg = (
                pf[3 * halves + h, rows(b), :] * out,
                back * feat[2 * halves + h, b],
                back * feat[halves + h, b],
            )
            result = []
            for s in range(3):
                fgs[s * halves + h, pl.ds(b, SUB, stride=block), :] = fg[s]
                for j in range(3):
                    result.append(sums[3 * s + j] + fg[s] * pf[s * halves + h, rows(b - j), :])
            return tuple(result)

        sums = lax.fori_loop(0, block, finish, (jnp.zeros((SUB, LANES), F32),) * 9)
        for e in range(9):
            unit = e * halves + h
            r1_out[unit // 3, unit % 3 : unit % 3 + 1, :] = jnp.sum(sums[e], axis=0, keepdims=True)
        for s in range(3):
            tail_out[2 * s : 2 * s + 2, h * LANES : (h + 1) * LANES] = fgs[s * halves + h, 0:2, :]

    sum_out = [send(r1_out.at[lax.rem(g + d, G)], r1_in.at[d], R_GROUP, d, at_group(d)) for d in range(1, G)]
    for copy in sum_out:
        copy.start()
    tail = send(tail_out, tail_in, TAIL, 0, at(ctx - 1))

    @pl.when(ctx > 0)
    def _():
        tail.start()

    r1_in[0] = r1_out[g]
    for h in range(halves):
        gated[:, h * LANES : (h + 1) * LANES] = gat[h].astype(gated.dtype)
    for copy in sum_out:
        copy.wait_recv()
    value = r1_in[lax.rem(g + G, G)]
    for i in range(1, G):
        value = value + r1_in[lax.rem(g - i + G, G)]
    r2_out[...] = value
    r2_in[0] = value
    line_sum = [send(r2_out, r2_in.at[d], R_LINE, d, at_line(d)) for d in range(1, lines)]
    for copy in line_sum:
        copy.start()

    @pl.when(ctx < count - 1)
    def _():
        tail.wait_recv()

    for h in range(halves):
        for s in range(3):
            fgs[s * halves + h, tokens : tokens + 2, :] = tail_in[2 * s : 2 * s + 2, h * LANES : (h + 1) * LANES]
    for h in range(halves):
        cols = slice(h * LANES, (h + 1) * LANES)
        for s in range(3):
            i = s * halves + h
            back = taps[s, 0:1, cols] * fgs[i, 0:tokens, :]
            back = back + taps[s, 1:2, cols] * fgs[i, 1 : tokens + 1, :]
            back = back + taps[s, 2:3, cols] * fgs[i, 2 : tokens + 2, :]
            grads[s, :, cols] = back.astype(grads.dtype)

    for copy in line_sum:
        copy.wait_recv()
    value = r2_in[lax.rem(z + lines, lines)]
    for i in range(1, lines):
        value = value + r2_in[lax.rem(z - i + lines, lines)]
    r3_out[...] = value
    r3_in[0] = value
    back_sum = [send(r3_out, r3_in.at[d], R_BACK, d, at_group(d)) for d in range(1, G)]
    for copy in back_sum:
        copy.start()
    for copy in back_sum:
        copy.wait_recv()
    blocks = [r3_in[lax.rem(g - i + G, G)] for i in range(G)]
    square = blocks[0] * blocks[0]
    for i in range(1, G):
        square = square + blocks[i] * blocks[i]
    r4_out[...] = square
    r4_in[0] = square
    norm_out = [send(r4_out, r4_in.at[d], NORM, d, at_tp(d)) for d in range(1, tp_size)]
    for copy in norm_out:
        copy.start()
    for copy in norm_out:
        copy.wait_recv()
    square = r4_in[lax.rem(tp + tp_size, tp_size)]
    for i in range(1, tp_size):
        square = square + r4_in[lax.rem(tp - i + tp_size, tp_size)]
    norm = jnp.sqrt(jnp.sum(jnp.sum(square, axis=0, keepdims=True), axis=1, keepdims=True))
    limit = bound[0]
    scale = limit / jnp.maximum(norm, limit)
    for s in range(3):
        for j in range(3):
            for h in range(halves):
                unit = (3 * s + j) * halves + h
                filt[s, j : j + 1, h * LANES : (h + 1) * LANES] = (
                    blocks[unit // 3][unit % 3 : unit % 3 + 1, :] * scale
                )

    for copy in group_out + back_out + sum_out + line_sum + back_sum + norm_out:
        copy.wait_send()
    for d in range(1, lines):
        @pl.when(zz + d < lines)
        def _():
            line_out[d - 1].wait_send()

    @pl.when(ctx < count - 1)
    def _():
        halo.wait_send()

    @pl.when(ctx > 0)
    def _():
        tail.wait_send()


def local(projected, short_filter, decay_rates, residues, output_grad, clip_bound):
    _, tokens, channels = projected.shape
    modes = decay_rates.shape[0]
    halves = channels // LANES
    block = tokens // SUB
    tp_size = lax.axis_size("tp")
    tile = pltpu.VMEM((SUB, LANES), F32)
    tiles = pltpu.VMEM((G, SUB, LANES), F32)
    edge = pltpu.VMEM((8, channels), F32)
    vmem = pl.BlockSpec(memory_space=pltpu.VMEM)
    return pl.pallas_call(
        functools.partial(kernel, modes, tp_size),
        out_shape=(
            jax.ShapeDtypeStruct((tokens, channels), jnp.bfloat16),
            jax.ShapeDtypeStruct((3, tokens, channels), jnp.bfloat16),
            jax.ShapeDtypeStruct(short_filter.shape, F32),
        ),
        in_specs=[vmem] * 5 + [pl.BlockSpec(memory_space=pltpu.SMEM)],
        out_specs=(vmem, vmem, vmem),
        scratch_shapes=[
            pltpu.VMEM((4 * halves, PAD + tokens, LANES), F32),
            pltpu.VMEM((3 * halves, block, SUB, LANES), F32),
            pltpu.VMEM((2 * halves, block, SUB, LANES), F32),
            pltpu.VMEM((2 * halves, block, SUB, LANES), F32),
            pltpu.VMEM((halves, modes, SUB, LANES), F32),
            pltpu.VMEM((halves, block, SUB, LANES), F32),
            pltpu.VMEM((2 * halves, modes, SUB, LANES), F32),
            pltpu.VMEM((G // 2, SUB, LANES), F32),
            pltpu.VMEM((halves, tokens, LANES), F32),
            pltpu.VMEM((3 * halves, tokens + 8, LANES), F32),
            edge, edge, edge, edge,
            tiles, tiles, tile, tiles, tiles, tiles,
            tiles, tiles, tile, tiles, tile, tiles, tile, tiles,
            pltpu.SemaphoreType.DMA((9, 8)),
            pltpu.SemaphoreType.DMA((9, 8)),
        ],
        compiler_params=pltpu.CompilerParams(
            collective_id=0, has_side_effects=True, vmem_limit_bytes=32 * 1024 * 1024
        ),
    )(projected, short_filter, decay_rates, residues, output_grad, clip_bound)


def solution(mesh):
    placed = (
        P(None, "ctx", "tp"),
        P(None, None, "tp"),
        P(None, "tp"),
        P(None, "tp"),
        P("ctx", "tp"),
        P(),
    )
    return jax.shard_map(
        local,
        mesh=mesh,
        in_specs=placed,
        out_specs=(P("ctx", "tp"), P(None, "ctx", "tp"), P(None, None, "tp")),
        check_vma=False,
    )
```

```python
import functools

import jax
import jax.numpy as jnp
from jax import lax
from jax.experimental import pallas as pl
from jax.experimental.pallas import tpu as pltpu
from jax.sharding import PartitionSpec as P

MESH = pl.DeviceIdType.MESH
F32 = jnp.float32
LANES = 128
SUB = 8
PAD = 8
G = 8
HALO, EDGE, S_GROUP, S_LINE, S_BACK, W_GROUP, R_GROUP, R_RING, R_PLANE, TAIL = range(10)
ROWS = 4
HI = 2


def loop(start, stop, unroll, body, carry):
    def some(i, carry):
        for k in range(unroll):
            carry = body(start + i * unroll + k, carry)
        return carry

    return lax.fori_loop(0, (stop - start) // unroll, some, carry)


def kernel(
    modes, tp_size,
    proj_hbm, taps_hbm, rates_hbm, weights_hbm, cot_hbm, bound,
    gated, grads, filt,
    proj, taps, rates, weights, cot, in_sem,
    pf, feat, xs, ys, lam, htab, excl, rown, wown, gat, fgs,
    halo_out, halo_in, edge_in, tail_out, tail_in,
    sa_out, sa_in, chunk, ga_out, ga_in, sb_out, sb_in, sc_out, sc_in,
    r1_out, r1_in, r2_out, r2_in, r3_out, r3_in,
    ssem, rsem,
):
    loads = [
        pltpu.make_async_copy(src, dst, in_sem.at[i])
        for i, (src, dst) in enumerate(
            ((proj_hbm, proj), (rates_hbm, rates), (taps_hbm, taps), (cot_hbm, cot), (weights_hbm, weights))
        )
    ]
    for load in loads:
        load.start()
    tokens = proj.shape[1]
    halves = proj.shape[2] // LANES
    block = tokens // SUB
    quarter = modes // (G // 2)
    ctx, tp = lax.axis_index("ctx"), lax.axis_index("tp")
    count = lax.axis_size("ctx")
    lines = count // G
    z, g = ctx // G, lax.rem(ctx, G)
    causal = g < G // 2
    zz = jnp.where(causal, z, lines - 1 - z)
    towards = jnp.where(causal, 1, -1)

    def at_group(d):
        return {"ctx": z * G + lax.rem(g + d, G), "tp": tp}

    x, hi = tp // HI, lax.rem(tp, HI)
    ring, planes = HI * lines, tp_size // HI
    zr = hi * lines + z

    def at_ring(d):
        there = lax.rem(zr + d, ring)
        return {"ctx": lax.rem(there, lines) * G + g, "tp": x * HI + there // lines}

    def at_plane(d, e):
        return {"ctx": z * G + lax.rem(g + d, G), "tp": lax.rem(x + e, planes) * HI + hi}

    plane = [(d, e) for e in range(planes) for d in range(G)]

    def at(c):
        return {"ctx": c, "tp": tp}

    halo_in[...] = jnp.zeros_like(halo_in)
    edge_in[...] = jnp.zeros_like(edge_in)
    tail_in[...] = jnp.zeros_like(tail_in)
    sb_in[...] = jnp.zeros_like(sb_in)

    barrier = pltpu.get_barrier_semaphore()
    for d in range(1, ring):
        pl.semaphore_signal(barrier, inc=1, device_id=at_ring(d), device_id_type=MESH)
    for d, e in plane[1:]:
        pl.semaphore_signal(barrier, inc=1, device_id=at_plane(d, e), device_id_type=MESH)
    ends, begins = jnp.logical_and(g == G - 1, z < lines - 1), z > 0

    @pl.when(ends)
    def _():
        for d in range(G - 1):
            pl.semaphore_signal(barrier, inc=1, device_id=at(ctx + 1 + d), device_id_type=MESH)

    @pl.when(jnp.logical_and(begins, g < G - 1))
    def _():
        pl.semaphore_signal(barrier, inc=1, device_id=at(z * G - 1), device_id_type=MESH)

    def send(src, dst, step, d, dev):
        return pltpu.make_async_remote_copy(
            src_ref=src, dst_ref=dst, send_sem=ssem.at[step, d], recv_sem=rsem.at[step, d],
            device_id=dev, device_id_type=MESH,
        )

    tail_out[...] = jnp.zeros_like(tail_out)
    r1_out[...] = jnp.zeros_like(r1_out)
    ga_out[...] = jnp.zeros_like(ga_out)
    halo_out[...] = jnp.zeros_like(halo_out)
    for load in loads:
        load.wait()

    for h in range(halves):
        cols = slice(h * LANES, (h + 1) * LANES)
        for s in range(3):
            pf[s * halves + h, 0:PAD, :] = jnp.zeros((PAD, LANES), F32)
            pf[s * halves + h, PAD : PAD + tokens, :] = proj[s, :, cols].astype(F32)
        pf[3 * halves + h, PAD : PAD + tokens, :] = cot[:, cols].astype(F32)

    for m in range(modes):
        rate = rates[m : m + 1, :]
        keep = jnp.exp(-rate)
        for h in range(halves):
            lam[h, m] = jnp.broadcast_to(keep[:, h * LANES : (h + 1) * LANES], (SUB, LANES))
            row = h * quarter + m % quarter
            rown[m // quarter, row : row + 1, :] = rate[:, h * LANES : (h + 1) * LANES]
            wown[m // quarter, row : row + 1, :] = weights[m : m + 1, h * LANES : (h + 1) * LANES]

    def rows(b):
        return pl.ds(PAD + b, SUB, stride=block)

    def tap(s, j, h):
        return jnp.broadcast_to(taps[s, j : j + 1, h * LANES : (h + 1) * LANES], (SUB, LANES))

    def featurize(b, h):
        f = []
        for s in range(3):
            i = s * halves + h
            value = tap(s, 0, h) * pf[i, rows(b), :]
            value = value + tap(s, 1, h) * pf[i, rows(b - 1), :]
            value = value + tap(s, 2, h) * pf[i, rows(b - 2), :]
            feat[i, b] = value
            f.append(value)
        xs[h, b] = f[1] * f[2]
        xs[halves + h, block - 1 - b] = pf[3 * halves + h, rows(b), :] * f[0]

    place = lax.broadcasted_iota(jnp.int32, (SUB, LANES), 0)
    inner = place >= 1
    for h in range(halves):
        loop(0, block, 4, lambda b, _: featurize(b, h), None)
        for b in range(2):
            xs[h, b] = jnp.where(inner, xs[h, b], 0.0)
            xs[halves + h, block - 1 - b] = jnp.where(inner, xs[halves + h, block - 1 - b], 0.0)

    for h in range(halves):
        cols = slice(h * LANES, (h + 1) * LANES)
        keeps = [lam[h, m] for m in range(modes)]

        def horner(b, state):
            front, back = xs[h, b], xs[halves + h, b]
            return tuple(
                state[2 * m + r] * keeps[m] + (front, back)[r] for m in range(modes) for r in range(2)
            )

        zero = jnp.zeros((SUB, LANES), F32)
        state = loop(0, block, 4, horner, (zero,) * (2 * modes))
        for m in range(modes):
            rate = rates[m : m + 1, cols]
            for r in range(2):
                value = state[2 * m + r]
                for k in (1, 2, 4):
                    fade = jnp.exp(-(block * k) * rate)
                    if r == 0:
                        value = value + jnp.where(place >= k, fade, 0.0) * pltpu.roll(value, k, 0)
                    else:
                        value = value + jnp.where(place < SUB - k, fade, 0.0) * pltpu.roll(value, SUB - k, 0)
                row = h * quarter + m % quarter
                owner = r * (G // 2) + m // quarter
                if r == 0:
                    excl[h, m] = jnp.where(place >= 1, pltpu.roll(value, 1, 0), 0.0)
                    sa_out[owner, row : row + 1, :] = value[SUB - 1 : SUB, :]
                else:
                    excl[halves + h, m] = jnp.where(place < SUB - 1, pltpu.roll(value, SUB - 1, 0), 0.0)
                    sa_out[owner, row : row + 1, :] = value[0:1, :]

    for h in range(halves):
        cols = slice(h * LANES, (h + 1) * LANES)

        def part(s, b):
            i = s * halves + h
            own = [taps[s, j : j + 1, cols] * pf[i, PAD + b - j : PAD + b - j + 1, :] for j in range(b + 1)]
            late = [
                taps[s, j : j + 1, cols] * pf[i, PAD + tokens + b - j : PAD + tokens + b - j + 1, :]
                for j in range(b + 1, 3)
            ]
            return sum(own[1:], own[0]), sum(late[1:], late[0])

        for s in range(3):
            halo_out[2 * s : 2 * s + 2, cols] = pf[s * halves + h, PAD + tokens - 2 : PAD + tokens, :]
        for b in range(2):
            q, k, v = (part(s, b) for s in range(3))
            other = pf[3 * halves + h, PAD + b : PAD + b + 1, :]
            none = jnp.zeros((1, LANES), F32)
            for owner in range(G):
                first, second = (k, v) if owner < G // 2 else ((other, none), q)
                for at_row, kind in ((SUB, 0), (2 * SUB, 1)):
                    row = at_row + b * halves + h
                    sa_out[owner, row : row + 1, :] = first[kind]
                    row = row + 2 * halves
                    sa_out[owner, row : row + 1, :] = second[kind]

    pl.semaphore_wait(
        barrier,
        (ring - 1) + (len(plane) - 1) + jnp.where(ends, G - 1, 0)
        + jnp.where(jnp.logical_and(begins, g < G - 1), 1, 0),
    )
    group_out = [send(sa_out.at[lax.rem(g + d, G)], sa_in.at[d], S_GROUP, d, at_group(d)) for d in range(1, G)]
    for copy in group_out:
        copy.start()
    edges = [
        send(sa_out.at[d, pl.ds(2 * SUB, SUB)], edge_in, EDGE, d, at((z + 1) * G + d)) for d in range(G)
    ]

    @pl.when(ends)
    def _():
        for copy in edges:
            copy.start()

    halo = send(halo_out, halo_in, HALO, 0, at(ctx + 1))

    @pl.when(ctx < count - 1)
    def _():
        halo.start()

    sa_in[0] = sa_out[g]

    chain = modes // 2
    for h in range(halves):
        cols = slice(h * LANES, (h + 1) * LANES)
        for first in range(0, modes, chain):
            keeps = [lam[h, m] for m in range(first, first + chain)]
            for s in range(3):
                def factor(b):
                    return pf[3 * halves + h, rows(b), :] if s == 0 else feat[(3 - s) * halves + h, b]

                def grow(b, state, mask=None):
                    b = block - 1 - b if s == 0 else b
                    with_ = factor(b)
                    if mask is not None:
                        with_ = jnp.where(mask, with_, 0.0)
                    result = []
                    for j in range(3):
                        u = with_ * pf[s * halves + h, rows(b - j), :]
                        result += [state[j * chain + m] * keeps[m] + u for m in range(chain)]
                    return tuple(result)

                state = (jnp.zeros((SUB, LANES), F32),) * (3 * chain)
                if s == 0:
                    state = loop(0, block - 2, 2, grow, state)
                    for b in range(block - 2, block):
                        state = grow(b, state, inner)
                else:
                    for b in range(2):
                        state = grow(b, state, inner)
                    state = loop(2, block, 2, grow, state)
                ahead = (place if s == 0 else SUB - 1 - place).astype(F32)
                for k in range(chain):
                    m = first + k
                    weight = jnp.exp(-(ahead * float(block) + 1.0) * rates[m : m + 1, cols]) * weights[m : m + 1, cols]
                    owner = (0 if s == 0 else G // 2) + m // quarter
                    row = h * quarter + m % quarter
                    for j in range(3):
                        index = j if s == 0 else 3 * (s - 1) + j
                        ga_out[owner, index, row : row + 1, :] = jnp.sum(
                            state[j * chain + k] * weight, axis=0, keepdims=True
                        )

    @pl.when(ctx > 0)
    def _():
        halo.wait_recv()

    for h in range(halves):
        for s in range(3):
            pf[s * halves + h, PAD - 2 : PAD, :] = halo_in[2 * s : 2 * s + 2, h * LANES : (h + 1) * LANES]
        for b in range(2):
            featurize(b, h)

    def both(row_of):
        return jnp.where(place < quarter, row_of(0), row_of(1))

    for q in range(G // 2):
        rate = rown[q]
        weight = wown[q]
        for s in range(3):
            for j in range(3):
                index = j if s == 0 else 3 * (s - 1) + j
                owner = (0 if s == 0 else G // 2) + q
                value = ga_out[owner, index]
                for b in range(2):
                    def product(h):
                        i = s * halves + h
                        if s == 0:
                            with_ = pf[3 * halves + h, PAD + b : PAD + b + 1, :]
                        else:
                            with_ = feat[(3 - s) * halves + h, b, 0:1, :]
                        return with_ * pf[i, PAD + b - j : PAD + b - j + 1, :]

                    power = float(b + 1 if s == 0 else tokens - b)
                    value = value + both(product) * (weight * jnp.exp(-power * rate))
                ga_out[owner, index] = value

    weight_out = [send(ga_out.at[lax.rem(g + d, G)], ga_in.at[d], W_GROUP, d, at_group(d)) for d in range(1, G)]

    for copy in group_out:
        copy.wait_recv()

    @pl.when(begins)
    def _():
        send(sa_out.at[0, pl.ds(2 * SUB, SUB)], edge_in, EDGE, g, at(ctx)).wait_recv()

    own_rate = rown[lax.rem(g, G // 2)]
    fade = jnp.exp(-float(tokens) * own_rate)
    fade_group = jnp.exp(-float(tokens * G) * own_rate)

    def member(i):
        return jnp.where(causal, i, G - 1 - i)

    factors = (
        jnp.where(causal, jnp.exp(-float(tokens - 1) * own_rate), 1.0),
        jnp.where(causal, jnp.exp(-float(tokens - 2) * own_rate), jnp.exp(-own_rate)),
    )
    for i in range(G):
        of = lax.rem(g - i + G, G)
        before = edge_in[...] if i == 0 else sa_in[lax.rem(g - i + 1 + G, G), 2 * SUB : 3 * SUB, :]
        pair = sa_in[of, SUB : 2 * SUB, :] + before
        pair = pair[0 : 2 * halves, :] * pair[2 * halves : 4 * halves, :]
        value = sa_in[of, 0:SUB, :]
        for b in range(2):
            value = value + factors[b] * both(lambda h: pair[b * halves + h : b * halves + h + 1, :])
        chunk[i] = value

    value = jnp.zeros((SUB, LANES), F32)
    for i in range(G):
        value = value * fade + chunk[member(i)]
    sb_out[...] = value
    line_out = [
        send(sb_out, sb_in.at[d], S_LINE, d, at((z + d * towards) * G + g)) for d in range(1, lines)
    ]
    for d in range(1, lines):
        @pl.when(zz + d < lines)
        def _():
            line_out[d - 1].start()

    for copy in weight_out:
        copy.start()
    ga_in[0] = ga_out[g]

    steps = lax.broadcasted_iota(jnp.int32, (block, LANES), 0).astype(F32)
    for h in range(halves):
        cols = slice(h * LANES, (h + 1) * LANES)
        total = jnp.zeros((block, LANES), F32)
        for m in range(modes):
            total = total + weights[m : m + 1, cols] * jnp.exp(-rates[m : m + 1, cols] * steps)
        for k in range(block):
            htab[h, k] = jnp.broadcast_to(total[k : k + 1, :], (SUB, LANES))

    def direct(hd, _):
        h = lax.rem(hd, halves)
        width = 8
        for b0 in range(0, block, width):
            acc = [None] * width
            for a0 in range(0, b0 + width, width):
                for a in range(a0, a0 + width):
                    x = xs[hd, a]
                    for i in range(width):
                        if b0 + i >= a:
                            term = htab[h, b0 + i - a] * x
                            acc[i] = term if acc[i] is None else acc[i] + term
            for i in range(width):
                ys[hd, b0 + i] = acc[i]

    lax.fori_loop(0, 2 * halves, direct, None)

    def readout(h, r, left):
        keeps = [lam[h, m] for m in range(modes)]

        def step(b, left):
            parts = list(left)
            while len(parts) > 1:
                parts = [parts[i] + parts[i + 1] for i in range(0, len(parts), 2)]
            ys[r * halves + h, b] = ys[r * halves + h, b] + parts[0]
            return tuple(left[m] * keeps[m] for m in range(modes))

        loop(0, block, 4, step, tuple(left))

    for h in range(halves):
        cols = slice(h * LANES, (h + 1) * LANES)
        for r in range(2):
            left = []
            for m in range(modes):
                value = excl[r * halves + h, m]
                if r == 0:
                    rate = rates[m : m + 1, cols]
                    behind = jnp.maximum(place - 1, 0).astype(F32) * float(block)
                    late = jnp.exp(-float(block - 1) * rate) * xs[h, 0, 0:1, :]
                    late = late + jnp.exp(-float(block - 2) * rate) * xs[h, 1, 0:1, :]
                    value = value + jnp.where(inner, jnp.exp(-behind * rate) * late, 0.0)
                left.append(value * (weights[m : m + 1, cols] * lam[h, m]))
            readout(h, r, left)

    def feature_grads(b, h):
        out, back = ys[h, b], ys[halves + h, block - 1 - b]
        return out, (
            pf[3 * halves + h, rows(b), :] * out,
            back * feat[2 * halves + h, b],
            back * feat[halves + h, b],
        )

    for h in range(halves):
        def gather(b, sums):
            _, fg = feature_grads(b, h)
            return tuple(
                sums[3 * s + j] + fg[s] * pf[s * halves + h, rows(b - j), :] for s in range(3) for j in range(3)
            )

        sums = loop(0, block, 4, gather, (jnp.zeros((SUB, LANES), F32),) * 9)
        for e in range(9):
            unit = e * halves + h
            r1_out[unit // 3, unit % 3 : unit % 3 + 1, :] = jnp.sum(sums[e], axis=0, keepdims=True)

    for d in range(1, lines):
        @pl.when(zz - d >= 0)
        def _():
            line_out[d - 1].wait_recv()

    value = jnp.zeros((SUB, LANES), F32)
    for d in range(lines - 1, 0, -1):
        value = value * fade_group + sb_in[d]
    for i in range(G):
        sc_out[member(i)] = value
        value = value * fade + chunk[member(i)]
    back_out = [send(sc_out.at[lax.rem(g + d, G)], sc_in.at[d], S_BACK, d, at_group(d)) for d in range(1, G)]
    for copy in back_out:
        copy.start()
    sc_in[0] = sc_out[g]
    for copy in weight_out:
        copy.wait_recv()

    for index in range(6):
        value = jnp.zeros((SUB, LANES), F32)
        for i in range(G):
            value = value + sc_out[i] * ga_in[lax.rem(g - i + G, G), index]
        for h in range(halves):
            total = jnp.sum(value[h * quarter : (h + 1) * quarter, :], axis=0, keepdims=True)
            for here, e in ((causal, index), (jnp.logical_not(causal), index + 3)):
                if e == index and index >= 3:
                    continue
                unit = e * halves + h
                row = unit % 3
                r1_out[unit // 3, row : row + 1, :] = r1_out[unit // 3, row : row + 1, :] + jnp.where(here, total, 0.0)
    sum_out = [send(r1_out.at[lax.rem(g + d, G)], r1_in.at[d], R_GROUP, d, at_group(d)) for d in range(1, G)]
    for copy in sum_out:
        copy.start()
    r1_in[0] = r1_out[g]
    for copy in sum_out:
        copy.wait_recv()
    value = r1_in[lax.rem(g + G, G)]
    for i in range(1, G):
        value = value + r1_in[lax.rem(g - i + G, G)]
    r2_out[...] = value
    r2_in[0] = value
    ring_out = [
        send(r2_out.at[pl.ds(0, ROWS)], r2_in.at[d, pl.ds(0, ROWS)], R_RING, d, at_ring(d)) for d in range(1, ring)
    ]
    for copy in ring_out:
        copy.start()

    for copy in back_out:
        copy.wait_recv()
    for h in range(halves):
        cols = slice(h * LANES, (h + 1) * LANES)
        for r in range(2):
            ahead = (place if r == 0 else SUB - 1 - place).astype(F32)
            left = []
            for m in range(modes):
                owner = r * (G // 2) + m // quarter
                row = h * quarter + m % quarter
                carry = sc_in[lax.rem(g - owner + G, G), row : row + 1, :]
                value = jnp.exp(-(float(block) * ahead + 1.0) * rates[m : m + 1, cols])
                left.append(value * (weights[m : m + 1, cols] * carry))
            readout(h, r, left)

    for h in range(halves):
        def finish(b, _):
            out, fg = feature_grads(b, h)
            gat[h, pl.ds(b, SUB, stride=block), :] = feat[h, b] * out
            for s in range(3):
                fgs[s * halves + h, pl.ds(b, SUB, stride=block), :] = fg[s]

        loop(0, block, 4, finish, None)
        for s in range(3):
            tail_out[2 * s : 2 * s + 2, h * LANES : (h + 1) * LANES] = fgs[s * halves + h, 0:2, :]
    tail = send(tail_out, tail_in, TAIL, 0, at(ctx - 1))

    @pl.when(ctx > 0)
    def _():
        tail.start()

    for h in range(halves):
        gated[:, h * LANES : (h + 1) * LANES] = gat[h].astype(gated.dtype)

    @pl.when(ctx < count - 1)
    def _():
        tail.wait_recv()

    for h in range(halves):
        for s in range(3):
            fgs[s * halves + h, tokens : tokens + 2, :] = tail_in[2 * s : 2 * s + 2, h * LANES : (h + 1) * LANES]
    for h in range(halves):
        cols = slice(h * LANES, (h + 1) * LANES)
        for s in range(3):
            i = s * halves + h
            back = taps[s, 0:1, cols] * fgs[i, 0:tokens, :]
            back = back + taps[s, 1:2, cols] * fgs[i, 1 : tokens + 1, :]
            back = back + taps[s, 2:3, cols] * fgs[i, 2 : tokens + 2, :]
            grads[s, :, cols] = back.astype(grads.dtype)

    for copy in ring_out:
        copy.wait_recv()

    def whole(part):
        value = r2_in[lax.rem(zr - part * lines + ring, ring), 0:ROWS, :]
        for i in range(1, lines):
            value = value + r2_in[lax.rem(zr - part * lines - i + ring, ring), 0:ROWS, :]
        return value

    square = jnp.zeros((1, LANES), F32)
    for part in range(HI):
        value = whole(part)
        square = square + jnp.sum((value * value)[0 : ROWS - 1, :], axis=0, keepdims=True)
    r3_out[...] = whole(hi)
    r3_out[ROWS - 1 : ROWS, :] = square
    r3_in[0] = r3_out[...]
    plane_out = [
        send(r3_out, r3_in.at[i], R_PLANE, i, at_plane(d, e)) for i, (d, e) in enumerate(plane) if i > 0
    ]
    for copy in plane_out:
        copy.start()
    for copy in plane_out:
        copy.wait_recv()

    def from_plane(i, k):
        return r3_in[lax.rem(x - k + planes, planes) * G + lax.rem(g - i + G, G)]

    blocks = [from_plane(i, x) for i in range(G)]
    square = jnp.zeros((1, LANES), F32)
    for k in range(planes):
        for i in range(G):
            square = square + from_plane(i, k)[ROWS - 1 : ROWS, :]
    norm = jnp.sqrt(jnp.sum(square, axis=1, keepdims=True))
    limit = bound[0]
    scale = limit / jnp.maximum(norm, limit)
    for s in range(3):
        for j in range(3):
            for h in range(halves):
                unit = (3 * s + j) * halves + h
                filt[s, j : j + 1, h * LANES : (h + 1) * LANES] = (
                    blocks[unit // 3][unit % 3 : unit % 3 + 1, :] * scale
                )

    for copy in group_out + weight_out + back_out + sum_out + ring_out + plane_out:
        copy.wait_send()
    for d in range(1, lines):
        @pl.when(zz + d < lines)
        def _():
            line_out[d - 1].wait_send()

    @pl.when(ends)
    def _():
        for copy in edges:
            copy.wait_send()

    @pl.when(ctx < count - 1)
    def _():
        halo.wait_send()

    @pl.when(ctx > 0)
    def _():
        tail.wait_send()


def local(projected, short_filter, decay_rates, residues, output_grad, clip_bound):
    _, tokens, channels = projected.shape
    modes = decay_rates.shape[0]
    halves = channels // LANES
    block = tokens // SUB
    tp_size = lax.axis_size("tp")
    lines, planes = lax.axis_size("ctx") // G, tp_size // HI
    tile = pltpu.VMEM((SUB, LANES), F32)
    tiles = pltpu.VMEM((G, SUB, LANES), F32)
    edge = pltpu.VMEM((8, channels), F32)
    vmem = pl.BlockSpec(memory_space=pltpu.VMEM)
    return pl.pallas_call(
        functools.partial(kernel, modes, tp_size),
        out_shape=(
            jax.ShapeDtypeStruct((tokens, channels), jnp.bfloat16),
            jax.ShapeDtypeStruct((3, tokens, channels), jnp.bfloat16),
            jax.ShapeDtypeStruct(short_filter.shape, F32),
        ),
        in_specs=[pl.BlockSpec(memory_space=pltpu.HBM)] * 5 + [pl.BlockSpec(memory_space=pltpu.SMEM)],
        out_specs=(vmem, vmem, vmem),
        scratch_shapes=[
            pltpu.VMEM(projected.shape, projected.dtype),
            pltpu.VMEM(short_filter.shape, F32),
            pltpu.VMEM(decay_rates.shape, F32),
            pltpu.VMEM(residues.shape, F32),
            pltpu.VMEM(output_grad.shape, output_grad.dtype),
            pltpu.SemaphoreType.DMA((5,)),
            pltpu.VMEM((4 * halves, PAD + tokens, LANES), F32),
            pltpu.VMEM((3 * halves, block, SUB, LANES), F32),
            pltpu.VMEM((2 * halves, block, SUB, LANES), F32),
            pltpu.VMEM((2 * halves, block, SUB, LANES), F32),
            pltpu.VMEM((halves, modes, SUB, LANES), F32),
            pltpu.VMEM((halves, block, SUB, LANES), F32),
            pltpu.VMEM((2 * halves, modes, SUB, LANES), F32),
            pltpu.VMEM((G // 2, SUB, LANES), F32),
            pltpu.VMEM((G // 2, SUB, LANES), F32),
            pltpu.VMEM((halves, tokens, LANES), F32),
            pltpu.VMEM((3 * halves, tokens + 8, LANES), F32),
            edge, edge, tile, edge, edge,
            pltpu.VMEM((G, 3 * SUB, LANES), F32), pltpu.VMEM((G, 3 * SUB, LANES), F32), tiles,
            pltpu.VMEM((G, 6, SUB, LANES), F32), pltpu.VMEM((G, 6, SUB, LANES), F32),
            tile, tiles, tiles, tiles,
            tiles, tiles, tile, pltpu.VMEM((HI * lines, SUB, LANES), F32),
            pltpu.VMEM((ROWS, LANES), F32), pltpu.VMEM((G * planes, ROWS, LANES), F32),
            pltpu.SemaphoreType.DMA((10, 32)),
            pltpu.SemaphoreType.DMA((10, 32)),
        ],
        compiler_params=pltpu.CompilerParams(
            collective_id=0, has_side_effects=True, vmem_limit_bytes=32 * 1024 * 1024
        ),
    )(projected, short_filter, decay_rates, residues, output_grad, clip_bound)


def solution(mesh):
    placed = (
        P(None, "ctx", "tp"),
        P(None, None, "tp"),
        P(None, "tp"),
        P(None, "tp"),
        P("ctx", "tp"),
        P(),
    )
    return jax.shard_map(
        local,
        mesh=mesh,
        in_specs=placed,
        out_specs=(P("ctx", "tp"), P(None, "ctx", "tp"), P(None, None, "tp")),
        check_vma=False,
    )
```

```python
import functools

import jax
import jax.numpy as jnp
from jax import lax
from jax.experimental import pallas as pl
from jax.experimental.pallas import tpu as pltpu
from jax.sharding import PartitionSpec as P

MESH = pl.DeviceIdType.MESH
F32 = jnp.float32
LANES = 128
SUB = 8
PAD = 8
G = 8
HALO, EDGE, S_GROUP, S_LINE, S_BACK, W_GROUP, R_GROUP, R_RING, R_PLANE, TAIL = range(10)
ROWS = 4
HI = 2


def loop(start, stop, unroll, body, carry):
    def some(i, carry):
        for k in range(unroll):
            carry = body(start + i * unroll + k, carry)
        return carry

    return lax.fori_loop(0, (stop - start) // unroll, some, carry)


def kernel(
    modes, tp_size,
    proj_hbm, taps_hbm, rates_hbm, weights_hbm, cot_hbm, bound,
    gated, grads, filt,
    proj, taps, rates, weights, cot, in_sem,
    pf, ps, feat, xs, ys, lam, htab, excl, rown, wown, gat, fgs,
    halo_out, halo_in, edge_in, tail_out, tail_in,
    sa_out, sa_in, chunk, ga_out, ga_in, sb_out, sb_in, sc_out, sc_in,
    r1_out, r1_in, r2_out, r2_in, r3_out, r3_in,
    ssem, rsem,
):
    loads = [
        pltpu.make_async_copy(src, dst, in_sem.at[i])
        for i, (src, dst) in enumerate(
            ((proj_hbm, proj), (rates_hbm, rates), (taps_hbm, taps), (cot_hbm, cot), (weights_hbm, weights))
        )
    ]
    for load in loads:
        load.start()
    tokens = proj.shape[1]
    halves = proj.shape[2] // LANES
    block = tokens // SUB
    quarter = modes // (G // 2)
    ctx, tp = lax.axis_index("ctx"), lax.axis_index("tp")
    count = lax.axis_size("ctx")
    lines = count // G
    z, g = ctx // G, lax.rem(ctx, G)
    causal = g < G // 2
    zz = jnp.where(causal, z, lines - 1 - z)
    towards = jnp.where(causal, 1, -1)

    def at_group(d):
        return {"ctx": z * G + lax.rem(g + d, G), "tp": tp}

    x, hi = tp // HI, lax.rem(tp, HI)
    ring, planes = HI * lines, tp_size // HI
    zr = hi * lines + z

    def at_ring(d):
        there = lax.rem(zr + d, ring)
        return {"ctx": lax.rem(there, lines) * G + g, "tp": x * HI + there // lines}

    def at_plane(d, e):
        return {"ctx": z * G + lax.rem(g + d, G), "tp": lax.rem(x + e, planes) * HI + hi}

    plane = [(d, e) for e in range(planes) for d in range(G)]

    def at(c):
        return {"ctx": c, "tp": tp}

    halo_in[...] = jnp.zeros_like(halo_in)
    edge_in[...] = jnp.zeros_like(edge_in)
    tail_in[...] = jnp.zeros_like(tail_in)
    sb_in[...] = jnp.zeros_like(sb_in)

    barrier = pltpu.get_barrier_semaphore()
    for d in range(1, ring):
        pl.semaphore_signal(barrier, inc=1, device_id=at_ring(d), device_id_type=MESH)
    for d, e in plane[1:]:
        pl.semaphore_signal(barrier, inc=1, device_id=at_plane(d, e), device_id_type=MESH)
    ends, begins = jnp.logical_and(g == G - 1, z < lines - 1), z > 0

    @pl.when(ends)
    def _():
        for d in range(G - 1):
            pl.semaphore_signal(barrier, inc=1, device_id=at(ctx + 1 + d), device_id_type=MESH)

    @pl.when(jnp.logical_and(begins, g < G - 1))
    def _():
        pl.semaphore_signal(barrier, inc=1, device_id=at(z * G - 1), device_id_type=MESH)

    def send(src, dst, step, d, dev):
        return pltpu.make_async_remote_copy(
            src_ref=src, dst_ref=dst, send_sem=ssem.at[step, d], recv_sem=rsem.at[step, d],
            device_id=dev, device_id_type=MESH,
        )

    tail_out[...] = jnp.zeros_like(tail_out)
    r1_out[...] = jnp.zeros_like(r1_out)
    ga_out[...] = jnp.zeros_like(ga_out)
    halo_out[...] = jnp.zeros_like(halo_out)
    for load in loads:
        load.wait()

    for h in range(halves):
        cols = slice(h * LANES, (h + 1) * LANES)
        for s in range(3):
            pf[s * halves + h, 0:PAD, :] = jnp.zeros((PAD, LANES), F32)
            pf[s * halves + h, PAD : PAD + tokens, :] = proj[s, :, cols].astype(F32)
        pf[3 * halves + h, PAD : PAD + tokens, :] = cot[:, cols].astype(F32)

    for m in range(modes):
        rate = rates[m : m + 1, :]
        keep = jnp.exp(-rate)
        for h in range(halves):
            lam[h, m] = jnp.broadcast_to(keep[:, h * LANES : (h + 1) * LANES], (SUB, LANES))
            row = h * quarter + m % quarter
            rown[m // quarter, row : row + 1, :] = rate[:, h * LANES : (h + 1) * LANES]
            wown[m // quarter, row : row + 1, :] = weights[m : m + 1, h * LANES : (h + 1) * LANES]

    def rows(b):
        return pl.ds(PAD + b, SUB, stride=block)

    def tap(s, j, h):
        return jnp.broadcast_to(taps[s, j : j + 1, h * LANES : (h + 1) * LANES], (SUB, LANES))

    def featurize(b, h):
        f = []
        for s in range(3):
            i = s * halves + h
            value = tap(s, 0, h) * ps[i, b + 2]
            value = value + tap(s, 1, h) * ps[i, b + 1]
            value = value + tap(s, 2, h) * ps[i, b]
            feat[i, b] = value
            f.append(value)
        xs[h, b] = f[1] * f[2]
        xs[halves + h, block - 1 - b] = ps[3 * halves + h, b + 2] * f[0]

    def turn(i, b):
        ps[i, b + 2] = pf[i, rows(b), :]

    for i in range(4 * halves):
        if i < 3 * halves:
            turn(i, -2)
            turn(i, -1)
        loop(0, block, 8, lambda b, _: turn(i, b), None)

    place = lax.broadcasted_iota(jnp.int32, (SUB, LANES), 0)
    inner = place >= 1
    for h in range(halves):
        loop(0, block, 4, lambda b, _: featurize(b, h), None)
        for b in range(2):
            xs[h, b] = jnp.where(inner, xs[h, b], 0.0)
            xs[halves + h, block - 1 - b] = jnp.where(inner, xs[halves + h, block - 1 - b], 0.0)

    for h in range(halves):
        cols = slice(h * LANES, (h + 1) * LANES)
        keeps = [lam[h, m] for m in range(modes)]

        def horner(b, state):
            front, back = xs[h, b], xs[halves + h, b]
            return tuple(
                state[2 * m + r] * keeps[m] + (front, back)[r] for m in range(modes) for r in range(2)
            )

        zero = jnp.zeros((SUB, LANES), F32)
        state = loop(0, block, 4, horner, (zero,) * (2 * modes))
        for m in range(modes):
            rate = rates[m : m + 1, cols]
            for r in range(2):
                value = state[2 * m + r]
                for k in (1, 2, 4):
                    fade = jnp.exp(-(block * k) * rate)
                    if r == 0:
                        value = value + jnp.where(place >= k, fade, 0.0) * pltpu.roll(value, k, 0)
                    else:
                        value = value + jnp.where(place < SUB - k, fade, 0.0) * pltpu.roll(value, SUB - k, 0)
                row = h * quarter + m % quarter
                owner = r * (G // 2) + m // quarter
                if r == 0:
                    excl[h, m] = jnp.where(place >= 1, pltpu.roll(value, 1, 0), 0.0)
                    sa_out[owner, row : row + 1, :] = value[SUB - 1 : SUB, :]
                else:
                    excl[halves + h, m] = jnp.where(place < SUB - 1, pltpu.roll(value, SUB - 1, 0), 0.0)
                    sa_out[owner, row : row + 1, :] = value[0:1, :]

    for h in range(halves):
        cols = slice(h * LANES, (h + 1) * LANES)

        def part(s, b):
            i = s * halves + h
            own = [taps[s, j : j + 1, cols] * pf[i, PAD + b - j : PAD + b - j + 1, :] for j in range(b + 1)]
            late = [
                taps[s, j : j + 1, cols] * pf[i, PAD + tokens + b - j : PAD + tokens + b - j + 1, :]
                for j in range(b + 1, 3)
            ]
            return sum(own[1:], own[0]), sum(late[1:], late[0])

        for s in range(3):
            halo_out[2 * s : 2 * s + 2, cols] = pf[s * halves + h, PAD + tokens - 2 : PAD + tokens, :]
        for b in range(2):
            q, k, v = (part(s, b) for s in range(3))
            other = pf[3 * halves + h, PAD + b : PAD + b + 1, :]
            none = jnp.zeros((1, LANES), F32)
            for owner in range(G):
                first, second = (k, v) if owner < G // 2 else ((other, none), q)
                for at_row, kind in ((SUB, 0), (2 * SUB, 1)):
                    row = at_row + b * halves + h
                    sa_out[owner, row : row + 1, :] = first[kind]
                    row = row + 2 * halves
                    sa_out[owner, row : row + 1, :] = second[kind]

    chain = modes // 2
    def grown(h, first):
        cols = slice(h * LANES, (h + 1) * LANES)
        keeps = [lam[h, m] for m in range(first, first + chain)]
        for s in range(3):
            def factor(b):
                return ps[3 * halves + h, b + 2] if s == 0 else feat[(3 - s) * halves + h, b]

            def grow(b, state, mask=None):
                b = block - 1 - b if s == 0 else b
                with_ = factor(b)
                if mask is not None:
                    with_ = jnp.where(mask, with_, 0.0)
                result = []
                for j in range(3):
                    u = with_ * ps[s * halves + h, b + 2 - j]
                    result += [state[j * chain + m] * keeps[m] + u for m in range(chain)]
                return tuple(result)

            state = (jnp.zeros((SUB, LANES), F32),) * (3 * chain)
            if s == 0:
                state = loop(0, block - 2, 2, grow, state)
                for b in range(block - 2, block):
                    state = grow(b, state, inner)
            else:
                for b in range(2):
                    state = grow(b, state, inner)
                state = loop(2, block, 2, grow, state)
            ahead = (place if s == 0 else SUB - 1 - place).astype(F32)
            for k in range(chain):
                m = first + k
                weight = jnp.exp(-(ahead * float(block) + 1.0) * rates[m : m + 1, cols]) * weights[m : m + 1, cols]
                owner = (0 if s == 0 else G // 2) + m // quarter
                row = h * quarter + m % quarter
                for j in range(3):
                    index = j if s == 0 else 3 * (s - 1) + j
                    ga_out[owner, index, row : row + 1, :] = jnp.sum(
                        state[j * chain + k] * weight, axis=0, keepdims=True
                    )

    pieces = [(h, first) for h in range(halves) for first in range(0, modes, chain)]
    for piece in pieces[:1]:
        grown(*piece)

    pl.semaphore_wait(
        barrier,
        (ring - 1) + (len(plane) - 1) + jnp.where(ends, G - 1, 0)
        + jnp.where(jnp.logical_and(begins, g < G - 1), 1, 0),
    )
    group_out = [send(sa_out.at[lax.rem(g + d, G)], sa_in.at[d], S_GROUP, d, at_group(d)) for d in range(1, G)]
    for copy in group_out:
        copy.start()
    edges = [
        send(sa_out.at[d, pl.ds(2 * SUB, SUB)], edge_in, EDGE, d, at((z + 1) * G + d)) for d in range(G)
    ]

    @pl.when(ends)
    def _():
        for copy in edges:
            copy.start()

    halo = send(halo_out, halo_in, HALO, 0, at(ctx + 1))

    @pl.when(ctx < count - 1)
    def _():
        halo.start()

    sa_in[0] = sa_out[g]

    for piece in pieces[1:4 - 1]:
        grown(*piece)

    def both(row_of):
        return jnp.where(place < quarter, row_of(0), row_of(1))

    for copy in group_out:
        copy.wait_recv()

    @pl.when(begins)
    def _():
        send(sa_out.at[0, pl.ds(2 * SUB, SUB)], edge_in, EDGE, g, at(ctx)).wait_recv()

    own_rate = rown[lax.rem(g, G // 2)]
    fade = jnp.exp(-float(tokens) * own_rate)
    fade_group = jnp.exp(-float(tokens * G) * own_rate)

    def member(i):
        return jnp.where(causal, i, G - 1 - i)

    factors = (
        jnp.where(causal, jnp.exp(-float(tokens - 1) * own_rate), 1.0),
        jnp.where(causal, jnp.exp(-float(tokens - 2) * own_rate), jnp.exp(-own_rate)),
    )
    for i in range(G):
        of = lax.rem(g - i + G, G)
        before = edge_in[...] if i == 0 else sa_in[lax.rem(g - i + 1 + G, G), 2 * SUB : 3 * SUB, :]
        pair = sa_in[of, SUB : 2 * SUB, :] + before
        pair = pair[0 : 2 * halves, :] * pair[2 * halves : 4 * halves, :]
        value = sa_in[of, 0:SUB, :]
        for b in range(2):
            value = value + factors[b] * both(lambda h: pair[b * halves + h : b * halves + h + 1, :])
        chunk[i] = value

    value = jnp.zeros((SUB, LANES), F32)
    for i in range(G):
        value = value * fade + chunk[member(i)]
    sb_out[...] = value
    line_out = [
        send(sb_out, sb_in.at[d], S_LINE, d, at((z + d * towards) * G + g)) for d in range(1, lines)
    ]
    for d in range(1, lines):
        @pl.when(zz + d < lines)
        def _():
            line_out[d - 1].start()

    for piece in pieces[4 - 1:]:
        grown(*piece)

    @pl.when(ctx > 0)
    def _():
        halo.wait_recv()

    for h in range(halves):
        for s in range(3):
            pf[s * halves + h, PAD - 2 : PAD, :] = halo_in[2 * s : 2 * s + 2, h * LANES : (h + 1) * LANES]
            turn(s * halves + h, -2)
            turn(s * halves + h, -1)
        for b in range(2):
            featurize(b, h)

    for q in range(G // 2):
        rate = rown[q]
        weight = wown[q]
        for s in range(3):
            for j in range(3):
                index = j if s == 0 else 3 * (s - 1) + j
                owner = (0 if s == 0 else G // 2) + q
                value = ga_out[owner, index]
                for b in range(2):
                    def product(h):
                        i = s * halves + h
                        if s == 0:
                            with_ = pf[3 * halves + h, PAD + b : PAD + b + 1, :]
                        else:
                            with_ = feat[(3 - s) * halves + h, b, 0:1, :]
                        return with_ * pf[i, PAD + b - j : PAD + b - j + 1, :]

                    power = float(b + 1 if s == 0 else tokens - b)
                    value = value + both(product) * (weight * jnp.exp(-power * rate))
                ga_out[owner, index] = value

    weight_out = [send(ga_out.at[lax.rem(g + d, G)], ga_in.at[d], W_GROUP, d, at_group(d)) for d in range(1, G)]

    for copy in weight_out:
        copy.start()
    ga_in[0] = ga_out[g]

    steps = lax.broadcasted_iota(jnp.int32, (block, LANES), 0).astype(F32)
    for h in range(halves):
        cols = slice(h * LANES, (h + 1) * LANES)
        total = jnp.zeros((block, LANES), F32)
        for m in range(modes):
            total = total + weights[m : m + 1, cols] * jnp.exp(-rates[m : m + 1, cols] * steps)
        for k in range(block):
            htab[h, k] = jnp.broadcast_to(total[k : k + 1, :], (SUB, LANES))

    def direct(hd, _):
        h = lax.rem(hd, halves)
        width = 8
        for b0 in range(0, block, width):
            acc = [None] * width
            for a0 in range(0, b0 + width, width):
                for a in range(a0, a0 + width):
                    x = xs[hd, a]
                    for i in range(width):
                        if b0 + i >= a:
                            term = htab[h, b0 + i - a] * x
                            acc[i] = term if acc[i] is None else acc[i] + term
            for i in range(width):
                ys[hd, b0 + i] = acc[i]

    lax.fori_loop(0, 2 * halves, direct, None)

    def readout(h, r, left):
        keeps = [lam[h, m] for m in range(modes)]

        def step(b, left):
            parts = list(left)
            while len(parts) > 1:
                parts = [parts[i] + parts[i + 1] for i in range(0, len(parts), 2)]
            ys[r * halves + h, b] = ys[r * halves + h, b] + parts[0]
            return tuple(left[m] * keeps[m] for m in range(modes))

        loop(0, block, 4, step, tuple(left))

    for h in range(halves):
        cols = slice(h * LANES, (h + 1) * LANES)
        for r in range(2):
            left = []
            for m in range(modes):
                value = excl[r * halves + h, m]
                if r == 0:
                    rate = rates[m : m + 1, cols]
                    behind = jnp.maximum(place - 1, 0).astype(F32) * float(block)
                    late = jnp.exp(-float(block - 1) * rate) * xs[h, 0, 0:1, :]
                    late = late + jnp.exp(-float(block - 2) * rate) * xs[h, 1, 0:1, :]
                    value = value + jnp.where(inner, jnp.exp(-behind * rate) * late, 0.0)
                left.append(value * (weights[m : m + 1, cols] * lam[h, m]))
            readout(h, r, left)

    def feature_grads(b, h):
        out, back = ys[h, b], ys[halves + h, block - 1 - b]
        return out, (
            ps[3 * halves + h, b + 2] * out,
            back * feat[2 * halves + h, b],
            back * feat[halves + h, b],
        )

    for h in range(halves):
        def gather(b, sums):
            _, fg = feature_grads(b, h)
            return tuple(
                sums[3 * s + j] + fg[s] * ps[s * halves + h, b + 2 - j] for s in range(3) for j in range(3)
            )

        sums = loop(0, block, 4, gather, (jnp.zeros((SUB, LANES), F32),) * 9)
        for e in range(9):
            unit = e * halves + h
            r1_out[unit // 3, unit % 3 : unit % 3 + 1, :] = jnp.sum(sums[e], axis=0, keepdims=True)

    for d in range(1, lines):
        @pl.when(zz - d >= 0)
        def _():
            line_out[d - 1].wait_recv()

    value = jnp.zeros((SUB, LANES), F32)
    for d in range(lines - 1, 0, -1):
        value = value * fade_group + sb_in[d]
    for i in range(G):
        sc_out[member(i)] = value
        value = value * fade + chunk[member(i)]
    back_out = [send(sc_out.at[lax.rem(g + d, G)], sc_in.at[d], S_BACK, d, at_group(d)) for d in range(1, G)]
    for copy in back_out:
        copy.start()
    sc_in[0] = sc_out[g]
    for copy in weight_out:
        copy.wait_recv()

    for index in range(6):
        value = jnp.zeros((SUB, LANES), F32)
        for i in range(G):
            value = value + sc_out[i] * ga_in[lax.rem(g - i + G, G), index]
        for h in range(halves):
            total = jnp.sum(value[h * quarter : (h + 1) * quarter, :], axis=0, keepdims=True)
            for here, e in ((causal, index), (jnp.logical_not(causal), index + 3)):
                if e == index and index >= 3:
                    continue
                unit = e * halves + h
                row = unit % 3
                r1_out[unit // 3, row : row + 1, :] = r1_out[unit // 3, row : row + 1, :] + jnp.where(here, total, 0.0)
    sum_out = [send(r1_out.at[lax.rem(g + d, G)], r1_in.at[d], R_GROUP, d, at_group(d)) for d in range(1, G)]
    for copy in sum_out:
        copy.start()
    r1_in[0] = r1_out[g]
    for copy in sum_out:
        copy.wait_recv()
    value = r1_in[lax.rem(g + G, G)]
    for i in range(1, G):
        value = value + r1_in[lax.rem(g - i + G, G)]
    r2_out[...] = value
    r2_in[0] = value
    ring_out = [
        send(r2_out.at[pl.ds(0, ROWS)], r2_in.at[d, pl.ds(0, ROWS)], R_RING, d, at_ring(d)) for d in range(1, ring)
    ]
    for copy in ring_out:
        copy.start()

    for copy in back_out:
        copy.wait_recv()
    for h in range(halves):
        cols = slice(h * LANES, (h + 1) * LANES)
        for r in range(2):
            ahead = (place if r == 0 else SUB - 1 - place).astype(F32)
            left = []
            for m in range(modes):
                owner = r * (G // 2) + m // quarter
                row = h * quarter + m % quarter
                carry = sc_in[lax.rem(g - owner + G, G), row : row + 1, :]
                value = jnp.exp(-(float(block) * ahead + 1.0) * rates[m : m + 1, cols])
                left.append(value * (weights[m : m + 1, cols] * carry))
            readout(h, r, left)

    for h in range(halves):
        def finish(b, _):
            out, fg = feature_grads(b, h)
            gat[h, pl.ds(b, SUB, stride=block), :] = feat[h, b] * out
            for s in range(3):
                fgs[s * halves + h, pl.ds(b, SUB, stride=block), :] = fg[s]

        loop(0, block, 4, finish, None)
        for s in range(3):
            tail_out[2 * s : 2 * s + 2, h * LANES : (h + 1) * LANES] = fgs[s * halves + h, 0:2, :]
    tail = send(tail_out, tail_in, TAIL, 0, at(ctx - 1))

    @pl.when(ctx > 0)
    def _():
        tail.start()

    for h in range(halves):
        gated[:, h * LANES : (h + 1) * LANES] = gat[h].astype(gated.dtype)

    @pl.when(ctx < count - 1)
    def _():
        tail.wait_recv()

    for h in range(halves):
        for s in range(3):
            fgs[s * halves + h, tokens : tokens + 2, :] = tail_in[2 * s : 2 * s + 2, h * LANES : (h + 1) * LANES]
    for h in range(halves):
        cols = slice(h * LANES, (h + 1) * LANES)
        for s in range(3):
            i = s * halves + h
            back = taps[s, 0:1, cols] * fgs[i, 0:tokens, :]
            back = back + taps[s, 1:2, cols] * fgs[i, 1 : tokens + 1, :]
            back = back + taps[s, 2:3, cols] * fgs[i, 2 : tokens + 2, :]
            grads[s, :, cols] = back.astype(grads.dtype)

    for copy in ring_out:
        copy.wait_recv()

    def whole(part):
        value = r2_in[lax.rem(zr - part * lines + ring, ring), 0:ROWS, :]
        for i in range(1, lines):
            value = value + r2_in[lax.rem(zr - part * lines - i + ring, ring), 0:ROWS, :]
        return value

    square = jnp.zeros((1, LANES), F32)
    for part in range(HI):
        value = whole(part)
        square = square + jnp.sum((value * value)[0 : ROWS - 1, :], axis=0, keepdims=True)
    r3_out[...] = whole(hi)
    r3_out[ROWS - 1 : ROWS, :] = square
    r3_in[0] = r3_out[...]
    plane_out = [
        send(r3_out, r3_in.at[i], R_PLANE, i, at_plane(d, e)) for i, (d, e) in enumerate(plane) if i > 0
    ]
    for copy in plane_out:
        copy.start()
    for copy in plane_out:
        copy.wait_recv()

    def from_plane(i, k):
        return r3_in[lax.rem(x - k + planes, planes) * G + lax.rem(g - i + G, G)]

    blocks = [from_plane(i, x) for i in range(G)]
    square = jnp.zeros((1, LANES), F32)
    for k in range(planes):
        for i in range(G):
            square = square + from_plane(i, k)[ROWS - 1 : ROWS, :]
    norm = jnp.sqrt(jnp.sum(square, axis=1, keepdims=True))
    limit = bound[0]
    scale = limit / jnp.maximum(norm, limit)
    for s in range(3):
        for j in range(3):
            for h in range(halves):
                unit = (3 * s + j) * halves + h
                filt[s, j : j + 1, h * LANES : (h + 1) * LANES] = (
                    blocks[unit // 3][unit % 3 : unit % 3 + 1, :] * scale
                )

    for copy in group_out + weight_out + back_out + sum_out + ring_out + plane_out:
        copy.wait_send()
    for d in range(1, lines):
        @pl.when(zz + d < lines)
        def _():
            line_out[d - 1].wait_send()

    @pl.when(ends)
    def _():
        for copy in edges:
            copy.wait_send()

    @pl.when(ctx < count - 1)
    def _():
        halo.wait_send()

    @pl.when(ctx > 0)
    def _():
        tail.wait_send()


def local(projected, short_filter, decay_rates, residues, output_grad, clip_bound):
    _, tokens, channels = projected.shape
    modes = decay_rates.shape[0]
    halves = channels // LANES
    block = tokens // SUB
    tp_size = lax.axis_size("tp")
    lines, planes = lax.axis_size("ctx") // G, tp_size // HI
    tile = pltpu.VMEM((SUB, LANES), F32)
    tiles = pltpu.VMEM((G, SUB, LANES), F32)
    edge = pltpu.VMEM((8, channels), F32)
    vmem = pl.BlockSpec(memory_space=pltpu.VMEM)
    return pl.pallas_call(
        functools.partial(kernel, modes, tp_size),
        out_shape=(
            jax.ShapeDtypeStruct((tokens, channels), jnp.bfloat16),
            jax.ShapeDtypeStruct((3, tokens, channels), jnp.bfloat16),
            jax.ShapeDtypeStruct(short_filter.shape, F32),
        ),
        in_specs=[pl.BlockSpec(memory_space=pltpu.HBM)] * 5 + [pl.BlockSpec(memory_space=pltpu.SMEM)],
        out_specs=(vmem, vmem, vmem),
        scratch_shapes=[
            pltpu.VMEM(projected.shape, projected.dtype),
            pltpu.VMEM(short_filter.shape, F32),
            pltpu.VMEM(decay_rates.shape, F32),
            pltpu.VMEM(residues.shape, F32),
            pltpu.VMEM(output_grad.shape, output_grad.dtype),
            pltpu.SemaphoreType.DMA((5,)),
            pltpu.VMEM((4 * halves, PAD + tokens, LANES), F32),
            pltpu.VMEM((4 * halves, block + 2, SUB, LANES), F32),
            pltpu.VMEM((3 * halves, block, SUB, LANES), F32),
            pltpu.VMEM((2 * halves, block, SUB, LANES), F32),
            pltpu.VMEM((2 * halves, block, SUB, LANES), F32),
            pltpu.VMEM((halves, modes, SUB, LANES), F32),
            pltpu.VMEM((halves, block, SUB, LANES), F32),
            pltpu.VMEM((2 * halves, modes, SUB, LANES), F32),
            pltpu.VMEM((G // 2, SUB, LANES), F32),
            pltpu.VMEM((G // 2, SUB, LANES), F32),
            pltpu.VMEM((halves, tokens, LANES), F32),
            pltpu.VMEM((3 * halves, tokens + 8, LANES), F32),
            edge, edge, tile, edge, edge,
            pltpu.VMEM((G, 3 * SUB, LANES), F32), pltpu.VMEM((G, 3 * SUB, LANES), F32), tiles,
            pltpu.VMEM((G, 6, SUB, LANES), F32), pltpu.VMEM((G, 6, SUB, LANES), F32),
            tile, tiles, tiles, tiles,
            tiles, tiles, tile, pltpu.VMEM((HI * lines, SUB, LANES), F32),
            pltpu.VMEM((ROWS, LANES), F32), pltpu.VMEM((G * planes, ROWS, LANES), F32),
            pltpu.SemaphoreType.DMA((10, 32)),
            pltpu.SemaphoreType.DMA((10, 32)),
        ],
        compiler_params=pltpu.CompilerParams(
            collective_id=0, has_side_effects=True, vmem_limit_bytes=32 * 1024 * 1024
        ),
    )(*(pltpu.with_memory_space_constraint(v, pltpu.HBM) for v in (projected, short_filter, decay_rates, residues, output_grad)), clip_bound)


def solution(mesh):
    placed = (
        P(None, "ctx", "tp"),
        P(None, None, "tp"),
        P(None, "tp"),
        P(None, "tp"),
        P("ctx", "tp"),
        P(),
    )
    return jax.shard_map(
        local,
        mesh=mesh,
        in_specs=placed,
        out_specs=(P("ctx", "tp"), P(None, "ctx", "tp"), P(None, None, "tp")),
        check_vma=False,
    )
```

```python
import functools

import jax
import jax.numpy as jnp
from jax import lax
from jax.experimental import pallas as pl
from jax.experimental.pallas import tpu as pltpu
from jax.sharding import PartitionSpec as P

MESH = pl.DeviceIdType.MESH
F32 = jnp.float32
LANES = 128
SUB = 8
PAD = 8
G = 8
HALO, EDGE, S_GROUP, S_LINE, S_BACK, W_GROUP, R_GROUP, R_RING, R_PAIR, R_PLANE, TAIL = range(11)
CORES = 2
ROWS = 4
HI = 2


def loop(start, stop, unroll, body, carry):
    def some(i, carry):
        for k in range(unroll):
            carry = body(start + i * unroll + k, carry)
        return carry

    return lax.fori_loop(0, (stop - start) // unroll, some, carry)


def kernel(
    modes, tp_size,
    proj_hbm, taps_hbm, rates_hbm, weights_hbm, cot_hbm, bound,
    gated, grads, filt,
    proj, taps, rates, weights, cot, in_sem,
    pf, ps, feat, xs, ys, lam, htab, excl, rown, wown, gat, fgs,
    halo_out, halo_in, edge_in, tail_out, tail_in,
    sa_out, sa_in, chunk, ga_out, ga_in, sb_out, sb_in, sc_out, sc_in,
    r1_out, r1_in, r2_out, r2_in, r3_out, r3_in,
    ssem, rsem,
):
    loads = [
        pltpu.make_async_copy(src, dst, in_sem.at[i])
        for i, (src, dst) in enumerate(
            ((proj_hbm, proj), (rates_hbm, rates), (taps_hbm, taps), (cot_hbm, cot), (weights_hbm, weights))
        )
    ]
    for load in loads:
        load.start()
    tokens = proj.shape[1]
    halves = proj.shape[2] // LANES
    block = tokens // SUB
    quarter = modes // (G // 2)
    ctx, tp = lax.axis_index("ctx"), lax.axis_index("tp")
    count = lax.axis_size("ctx")
    lines = count // G
    z, g = ctx // G, lax.rem(ctx, G)
    causal = g < G // 2
    zz = jnp.where(causal, z, lines - 1 - z)
    towards = jnp.where(causal, 1, -1)

    def at_group(d):
        return {"ctx": z * G + lax.rem(g + d, G), "tp": tp}

    x, hi = tp // HI, lax.rem(tp, HI)
    ring, planes = HI * lines, tp_size // HI
    zr = hi * lines + z

    def at_ring(d):
        there = lax.rem(zr + d, ring)
        return {"ctx": lax.rem(there, lines) * G + g, "tp": x * HI + there // lines}

    chips = G // CORES
    y, core = g // CORES, lax.rem(g, CORES)
    twin = 1 - core

    def at_plane(i):
        there = lax.rem(y + lax.rem(i, chips), chips) * CORES + core
        return {"ctx": z * G + there, "tp": lax.rem(x + i // chips, planes) * HI + hi}

    plane = planes * chips

    def at(c):
        return {"ctx": c, "tp": tp}

    halo_in[...] = jnp.zeros_like(halo_in)
    edge_in[...] = jnp.zeros_like(edge_in)
    tail_in[...] = jnp.zeros_like(tail_in)
    sb_in[...] = jnp.zeros_like(sb_in)

    barrier = pltpu.get_barrier_semaphore()
    def greet(first, last, dev):
        def signal(d, _):
            pl.semaphore_signal(barrier, inc=1, device_id=dev(d), device_id_type=MESH)

        lax.fori_loop(first, last, signal, None)

    greet(1, ring, at_ring)
    greet(1, G, at_group)
    greet(chips, plane, at_plane)
    ends, begins = jnp.logical_and(g == G - 1, z < lines - 1), z > 0

    @pl.when(ends)
    def _():
        greet(0, G - 1, lambda d: at(ctx + 1 + d))

    @pl.when(jnp.logical_and(begins, g < G - 1))
    def _():
        pl.semaphore_signal(barrier, inc=1, device_id=at(z * G - 1), device_id_type=MESH)

    def send(src, dst, step, d, dev):
        return pltpu.make_async_remote_copy(
            src_ref=src, dst_ref=dst, send_sem=ssem.at[step, d], recv_sem=rsem.at[step, d],
            device_id=dev, device_id_type=MESH,
        )

    def fan(order, src, dst, step, dev):
        for d in order:
            send(src(d), dst(d), step, 0, dev(d)).start()

    def far_first(n):
        return sorted(range(1, n), key=lambda d: -min(d, n - d))

    def through(sems, step, ref):
        pltpu.make_async_copy(ref, ref, sems.at[step, 0]).wait()

    def member_of(d):
        return lax.rem(g + d, G)

    rest = pl.ds(1, G - 1)
    tail_out[...] = jnp.zeros_like(tail_out)
    r1_out[...] = jnp.zeros_like(r1_out)
    ga_out[...] = jnp.zeros_like(ga_out)
    halo_out[...] = jnp.zeros_like(halo_out)
    for load in loads:
        load.wait()

    for h in range(halves):
        cols = slice(h * LANES, (h + 1) * LANES)
        for s in range(3):
            pf[s * halves + h, 0:PAD, :] = jnp.zeros((PAD, LANES), F32)
            pf[s * halves + h, PAD : PAD + tokens, :] = proj[s, :, cols].astype(F32)
        pf[3 * halves + h, PAD : PAD + tokens, :] = cot[:, cols].astype(F32)

    for m in range(modes):
        rate = rates[m : m + 1, :]
        keep = jnp.exp(-rate)
        for h in range(halves):
            lam[h, m] = jnp.broadcast_to(keep[:, h * LANES : (h + 1) * LANES], (SUB, LANES))
            row = h * quarter + m % quarter
            rown[m // quarter, row : row + 1, :] = rate[:, h * LANES : (h + 1) * LANES]
            wown[m // quarter, row : row + 1, :] = weights[m : m + 1, h * LANES : (h + 1) * LANES]

    def rows(b):
        return pl.ds(PAD + b, SUB, stride=block)

    def tap(s, j, h):
        return jnp.broadcast_to(taps[s, j : j + 1, h * LANES : (h + 1) * LANES], (SUB, LANES))

    def featurize(b, h):
        f = []
        for s in range(3):
            i = s * halves + h
            value = tap(s, 0, h) * ps[i, b + 2]
            value = value + tap(s, 1, h) * ps[i, b + 1]
            value = value + tap(s, 2, h) * ps[i, b]
            feat[i, b] = value
            f.append(value)
        xs[h, b] = f[1] * f[2]
        xs[halves + h, block - 1 - b] = ps[3 * halves + h, b + 2] * f[0]

    def turn(i, b):
        ps[i, b + 2] = pf[i, rows(b), :]

    for i in range(4 * halves):
        if i < 3 * halves:
            turn(i, -2)
            turn(i, -1)
        loop(0, block, 8, lambda b, _: turn(i, b), None)

    place = lax.broadcasted_iota(jnp.int32, (SUB, LANES), 0)
    inner = place >= 1
    for h in range(halves):
        loop(0, block, 4, lambda b, _: featurize(b, h), None)
        for b in range(2):
            xs[h, b] = jnp.where(inner, xs[h, b], 0.0)
            xs[halves + h, block - 1 - b] = jnp.where(inner, xs[halves + h, block - 1 - b], 0.0)

    for h in range(halves):
        cols = slice(h * LANES, (h + 1) * LANES)
        keeps = [lam[h, m] for m in range(modes)]

        def horner(b, state):
            front, back = xs[h, b], xs[halves + h, b]
            return tuple(
                state[2 * m + r] * keeps[m] + (front, back)[r] for m in range(modes) for r in range(2)
            )

        zero = jnp.zeros((SUB, LANES), F32)
        state = loop(0, block, 4, horner, (zero,) * (2 * modes))
        for m in range(modes):
            rate = rates[m : m + 1, cols]
            for r in range(2):
                value = state[2 * m + r]
                for k in (1, 2, 4):
                    fade = jnp.exp(-(block * k) * rate)
                    if r == 0:
                        value = value + jnp.where(place >= k, fade, 0.0) * pltpu.roll(value, k, 0)
                    else:
                        value = value + jnp.where(place < SUB - k, fade, 0.0) * pltpu.roll(value, SUB - k, 0)
                row = h * quarter + m % quarter
                owner = r * (G // 2) + m // quarter
                if r == 0:
                    excl[h, m] = jnp.where(place >= 1, pltpu.roll(value, 1, 0), 0.0)
                    sa_out[owner, row : row + 1, :] = value[SUB - 1 : SUB, :]
                else:
                    excl[halves + h, m] = jnp.where(place < SUB - 1, pltpu.roll(value, SUB - 1, 0), 0.0)
                    sa_out[owner, row : row + 1, :] = value[0:1, :]

    for h in range(halves):
        cols = slice(h * LANES, (h + 1) * LANES)

        def part(s, b):
            i = s * halves + h
            own = [taps[s, j : j + 1, cols] * pf[i, PAD + b - j : PAD + b - j + 1, :] for j in range(b + 1)]
            late = [
                taps[s, j : j + 1, cols] * pf[i, PAD + tokens + b - j : PAD + tokens + b - j + 1, :]
                for j in range(b + 1, 3)
            ]
            return sum(own[1:], own[0]), sum(late[1:], late[0])

        for s in range(3):
            halo_out[2 * s : 2 * s + 2, cols] = pf[s * halves + h, PAD + tokens - 2 : PAD + tokens, :]
        for b in range(2):
            q, k, v = (part(s, b) for s in range(3))
            other = pf[3 * halves + h, PAD + b : PAD + b + 1, :]
            none = jnp.zeros((1, LANES), F32)
            for owner in range(G):
                first, second = (k, v) if owner < G // 2 else ((other, none), q)
                for at_row, kind in ((SUB, 0), (2 * SUB, 1)):
                    row = at_row + b * halves + h
                    sa_out[owner, row : row + 1, :] = first[kind]
                    row = row + 2 * halves
                    sa_out[owner, row : row + 1, :] = second[kind]

    chain = modes // 2
    def grown(h, first):
        cols = slice(h * LANES, (h + 1) * LANES)
        keeps = [lam[h, m] for m in range(first, first + chain)]
        for s in range(3):
            def factor(b):
                return ps[3 * halves + h, b + 2] if s == 0 else feat[(3 - s) * halves + h, b]

            def grow(b, state, mask=None):
                b = block - 1 - b if s == 0 else b
                with_ = factor(b)
                if mask is not None:
                    with_ = jnp.where(mask, with_, 0.0)
                result = []
                for j in range(3):
                    u = with_ * ps[s * halves + h, b + 2 - j]
                    result += [state[j * chain + m] * keeps[m] + u for m in range(chain)]
                return tuple(result)

            state = (jnp.zeros((SUB, LANES), F32),) * (3 * chain)
            if s == 0:
                state = loop(0, block - 2, 2, grow, state)
                for b in range(block - 2, block):
                    state = grow(b, state, inner)
            else:
                for b in range(2):
                    state = grow(b, state, inner)
                state = loop(2, block, 2, grow, state)
            ahead = (place if s == 0 else SUB - 1 - place).astype(F32)
            for k in range(chain):
                m = first + k
                weight = jnp.exp(-(ahead * float(block) + 1.0) * rates[m : m + 1, cols]) * weights[m : m + 1, cols]
                owner = (0 if s == 0 else G // 2) + m // quarter
                row = h * quarter + m % quarter
                for j in range(3):
                    index = j if s == 0 else 3 * (s - 1) + j
                    ga_out[owner, index, row : row + 1, :] = jnp.sum(
                        state[j * chain + k] * weight, axis=0, keepdims=True
                    )

    pieces = [(h, first) for h in range(halves) for first in range(0, modes, chain)]
    for piece in pieces[:1]:
        grown(*piece)

    pl.semaphore_wait(
        barrier,
        (ring - 1) + (G - 1) + (plane - chips) + jnp.where(ends, G - 1, 0)
        + jnp.where(jnp.logical_and(begins, g < G - 1), 1, 0),
    )
    fan(far_first(G), lambda d: sa_out.at[member_of(d)], lambda d: sa_in.at[d], S_GROUP, at_group)
    @pl.when(ends)
    def _():
        fan(
            range(G), lambda d: sa_out.at[d, pl.ds(2 * SUB, SUB)], lambda d: edge_in, EDGE,
            lambda d: at((z + 1) * G + d),
        )

    halo = send(halo_out, halo_in, HALO, 0, at(ctx + 1))

    @pl.when(ctx < count - 1)
    def _():
        halo.start()

    sa_in[0] = sa_out[g]

    for piece in pieces[1:4 - 1]:
        grown(*piece)

    def both(row_of):
        return jnp.where(place < quarter, row_of(0), row_of(1))

    through(rsem, S_GROUP, sa_in.at[rest])

    @pl.when(begins)
    def _():
        through(rsem, EDGE, edge_in)

    own_rate = rown[lax.rem(g, G // 2)]
    fade = jnp.exp(-float(tokens) * own_rate)
    fade_group = jnp.exp(-float(tokens * G) * own_rate)

    def member(i):
        return jnp.where(causal, i, G - 1 - i)

    factors = (
        jnp.where(causal, jnp.exp(-float(tokens - 1) * own_rate), 1.0),
        jnp.where(causal, jnp.exp(-float(tokens - 2) * own_rate), jnp.exp(-own_rate)),
    )
    for i in range(G):
        of = lax.rem(g - i + G, G)
        before = edge_in[...] if i == 0 else sa_in[lax.rem(g - i + 1 + G, G), 2 * SUB : 3 * SUB, :]
        pair = sa_in[of, SUB : 2 * SUB, :] + before
        pair = pair[0 : 2 * halves, :] * pair[2 * halves : 4 * halves, :]
        value = sa_in[of, 0:SUB, :]
        for b in range(2):
            value = value + factors[b] * both(lambda h: pair[b * halves + h : b * halves + h + 1, :])
        chunk[i] = value

    value = jnp.zeros((SUB, LANES), F32)
    for i in range(G):
        value = value * fade + chunk[member(i)]
    sb_out[...] = value
    def along(d):
        return send(sb_out, sb_in.at[d], S_LINE, d, at((z + d * towards) * G + g))

    def line_loop(last, act):
        lax.fori_loop(1, last, lambda d, _: act(along(last - d)), None)

    line_loop(lines - zz, lambda copy: copy.start())
    for piece in pieces[4 - 1:]:
        grown(*piece)

    @pl.when(ctx > 0)
    def _():
        halo.wait_recv()

    for h in range(halves):
        for s in range(3):
            pf[s * halves + h, PAD - 2 : PAD, :] = halo_in[2 * s : 2 * s + 2, h * LANES : (h + 1) * LANES]
            turn(s * halves + h, -2)
            turn(s * halves + h, -1)
        for b in range(2):
            featurize(b, h)

    for q in range(G // 2):
        rate = rown[q]
        weight = wown[q]
        for s in range(3):
            for j in range(3):
                index = j if s == 0 else 3 * (s - 1) + j
                owner = (0 if s == 0 else G // 2) + q
                value = ga_out[owner, index]
                for b in range(2):
                    def product(h):
                        i = s * halves + h
                        if s == 0:
                            with_ = pf[3 * halves + h, PAD + b : PAD + b + 1, :]
                        else:
                            with_ = feat[(3 - s) * halves + h, b, 0:1, :]
                        return with_ * pf[i, PAD + b - j : PAD + b - j + 1, :]

                    power = float(b + 1 if s == 0 else tokens - b)
                    value = value + both(product) * (weight * jnp.exp(-power * rate))
                ga_out[owner, index] = value


    fan(far_first(G), lambda d: ga_out.at[member_of(d)], lambda d: ga_in.at[d], W_GROUP, at_group)
    ga_in[0] = ga_out[g]

    steps = lax.broadcasted_iota(jnp.int32, (block, LANES), 0).astype(F32)
    for h in range(halves):
        cols = slice(h * LANES, (h + 1) * LANES)
        total = jnp.zeros((block, LANES), F32)
        for m in range(modes):
            total = total + weights[m : m + 1, cols] * jnp.exp(-rates[m : m + 1, cols] * steps)
        for k in range(block):
            htab[h, k] = jnp.broadcast_to(total[k : k + 1, :], (SUB, LANES))

    def direct(hd, _):
        h = lax.rem(hd, halves)
        width = 8
        for b0 in range(0, block, width):
            acc = [None] * width
            for a0 in range(0, b0 + width, width):
                for a in range(a0, a0 + width):
                    x = xs[hd, a]
                    for i in range(width):
                        if b0 + i >= a:
                            term = htab[h, b0 + i - a] * x
                            acc[i] = term if acc[i] is None else acc[i] + term
            for i in range(width):
                ys[hd, b0 + i] = acc[i]

    lax.fori_loop(0, 2 * halves, direct, None)

    def readout(h, r, left):
        keeps = [lam[h, m] for m in range(modes)]

        def step(b, left):
            parts = list(left)
            while len(parts) > 1:
                parts = [parts[i] + parts[i + 1] for i in range(0, len(parts), 2)]
            ys[r * halves + h, b] = ys[r * halves + h, b] + parts[0]
            return tuple(left[m] * keeps[m] for m in range(modes))

        loop(0, block, 4, step, tuple(left))

    for h in range(halves):
        cols = slice(h * LANES, (h + 1) * LANES)
        for r in range(2):
            left = []
            for m in range(modes):
                value = excl[r * halves + h, m]
                if r == 0:
                    rate = rates[m : m + 1, cols]
                    behind = jnp.maximum(place - 1, 0).astype(F32) * float(block)
                    late = jnp.exp(-float(block - 1) * rate) * xs[h, 0, 0:1, :]
                    late = late + jnp.exp(-float(block - 2) * rate) * xs[h, 1, 0:1, :]
                    value = value + jnp.where(inner, jnp.exp(-behind * rate) * late, 0.0)
                left.append(value * (weights[m : m + 1, cols] * lam[h, m]))
            readout(h, r, left)

    def feature_grads(b, h):
        out, back = ys[h, b], ys[halves + h, block - 1 - b]
        return out, (
            ps[3 * halves + h, b + 2] * out,
            back * feat[2 * halves + h, b],
            back * feat[halves + h, b],
        )

    for h in range(halves):
        def gather(b, sums):
            _, fg = feature_grads(b, h)
            return tuple(
                sums[3 * s + j] + fg[s] * ps[s * halves + h, b + 2 - j] for s in range(3) for j in range(3)
            )

        sums = loop(0, block, 4, gather, (jnp.zeros((SUB, LANES), F32),) * 9)
        for e in range(9):
            unit = e * halves + h
            r1_out[unit // 3, unit % 3 : unit % 3 + 1, :] = jnp.sum(sums[e], axis=0, keepdims=True)

    line_loop(zz + 1, lambda copy: copy.wait_recv())
    value = jnp.zeros((SUB, LANES), F32)
    for d in range(lines - 1, 0, -1):
        value = value * fade_group + sb_in[d]
    for i in range(G):
        sc_out[member(i)] = value
        value = value * fade + chunk[member(i)]
    fan(far_first(G), lambda d: sc_out.at[member_of(d)], lambda d: sc_in.at[d], S_BACK, at_group)
    sc_in[0] = sc_out[g]
    through(rsem, W_GROUP, ga_in.at[rest])

    for index in range(6):
        value = jnp.zeros((SUB, LANES), F32)
        for i in range(G):
            value = value + sc_out[i] * ga_in[lax.rem(g - i + G, G), index]
        for h in range(halves):
            total = jnp.sum(value[h * quarter : (h + 1) * quarter, :], axis=0, keepdims=True)
            for here, e in ((causal, index), (jnp.logical_not(causal), index + 3)):
                if e == index and index >= 3:
                    continue
                unit = e * halves + h
                row = unit % 3
                r1_out[unit // 3, row : row + 1, :] = r1_out[unit // 3, row : row + 1, :] + jnp.where(here, total, 0.0)
    fan(far_first(G), lambda d: r1_out.at[member_of(d)], lambda d: r1_in.at[d], R_GROUP, at_group)
    r1_in[0] = r1_out[g]
    through(rsem, R_GROUP, r1_in.at[rest])
    value = r1_in[lax.rem(g + G, G)]
    for i in range(1, G):
        value = value + r1_in[lax.rem(g - i + G, G)]
    r2_out[...] = value[0:ROWS, :]
    r2_in[0] = value[0:ROWS, :]
    fan(far_first(ring), lambda d: r2_out, lambda d: r2_in.at[d], R_RING, at_ring)

    through(rsem, S_BACK, sc_in.at[rest])
    for h in range(halves):
        cols = slice(h * LANES, (h + 1) * LANES)
        for r in range(2):
            ahead = (place if r == 0 else SUB - 1 - place).astype(F32)
            left = []
            for m in range(modes):
                owner = r * (G // 2) + m // quarter
                row = h * quarter + m % quarter
                carry = sc_in[lax.rem(g - owner + G, G), row : row + 1, :]
                value = jnp.exp(-(float(block) * ahead + 1.0) * rates[m : m + 1, cols])
                left.append(value * (weights[m : m + 1, cols] * carry))
            readout(h, r, left)

    for h in range(halves):
        def finish(b, _):
            out, fg = feature_grads(b, h)
            gat[h, pl.ds(b, SUB, stride=block), :] = feat[h, b] * out
            for s in range(3):
                fgs[s * halves + h, pl.ds(b, SUB, stride=block), :] = fg[s]

        loop(0, block, 4, finish, None)
        for s in range(3):
            tail_out[2 * s : 2 * s + 2, h * LANES : (h + 1) * LANES] = fgs[s * halves + h, 0:2, :]
    tail = send(tail_out, tail_in, TAIL, 0, at(ctx - 1))

    @pl.when(ctx > 0)
    def _():
        tail.start()

    for h in range(halves):
        gated[:, h * LANES : (h + 1) * LANES] = gat[h].astype(gated.dtype)

    @pl.when(ctx < count - 1)
    def _():
        tail.wait_recv()

    for h in range(halves):
        for s in range(3):
            fgs[s * halves + h, tokens : tokens + 2, :] = tail_in[2 * s : 2 * s + 2, h * LANES : (h + 1) * LANES]
    for h in range(halves):
        cols = slice(h * LANES, (h + 1) * LANES)
        for s in range(3):
            i = s * halves + h
            back = taps[s, 0:1, cols] * fgs[i, 0:tokens, :]
            back = back + taps[s, 1:2, cols] * fgs[i, 1 : tokens + 1, :]
            back = back + taps[s, 2:3, cols] * fgs[i, 2 : tokens + 2, :]
            grads[s, :, cols] = back.astype(grads.dtype)

    through(rsem, R_RING, r2_in.at[pl.ds(1, ring - 1)])

    def whole(part):
        value = r2_in[lax.rem(zr - part * lines + ring, ring)]
        for i in range(1, lines):
            value = value + r2_in[lax.rem(zr - part * lines - i + ring, ring)]
        return value

    square = jnp.zeros((1, LANES), F32)
    for part in range(HI):
        value = whole(part)
        square = square + jnp.sum((value * value)[0 : ROWS - 1, :], axis=0, keepdims=True)
    for c in range(CORES):
        @pl.when(core == c)
        def _():
            r3_out[c * ROWS : (c + 1) * ROWS, :] = whole(hi)
            r3_out[(c + 1) * ROWS - 1 : (c + 1) * ROWS, :] = square

    pair = send(
        r3_out.at[pl.ds(core * ROWS, ROWS)], r3_out.at[pl.ds(core * ROWS, ROWS)], R_PAIR, 0, at(z * G + y * CORES + twin)
    )
    pair.start()
    through(rsem, R_PAIR, r3_out.at[pl.ds(twin * ROWS, ROWS)])
    r3_in[0] = r3_out[...]
    across = sorted(
        range(1, plane), key=lambda i: -(min(i % chips, chips - i % chips) + min(i // chips, planes - i // chips))
    )
    fan(across, lambda i: r3_out, lambda i: r3_in.at[i], R_PLANE, at_plane)
    through(rsem, R_PLANE, r3_in.at[pl.ds(1, plane - 1)])

    def from_plane(i, k):
        return r3_in[lax.rem(x - k + planes, planes) * chips + lax.rem(y - i + chips, chips)]

    pairs = [from_plane(i, x) for i in range(chips)]
    blocks = [pairs[i // CORES][i % CORES * ROWS : (i % CORES + 1) * ROWS, :] for i in range(G)]
    square = jnp.zeros((1, LANES), F32)
    for k in range(planes):
        for i in range(chips):
            both_cores = from_plane(i, k)
            for c in range(CORES):
                square = square + both_cores[(c + 1) * ROWS - 1 : (c + 1) * ROWS, :]
    norm = jnp.sqrt(jnp.sum(square, axis=1, keepdims=True))
    limit = bound[0]
    scale = limit / jnp.maximum(norm, limit)
    for s in range(3):
        for j in range(3):
            for h in range(halves):
                unit = (3 * s + j) * halves + h
                filt[s, j : j + 1, h * LANES : (h + 1) * LANES] = (
                    blocks[unit // 3][unit % 3 : unit % 3 + 1, :] * scale
                )

    for step, ref in (
        (S_GROUP, sa_in), (W_GROUP, ga_in), (S_BACK, sc_in), (R_GROUP, r1_in),
    ):
        through(ssem, step, ref.at[rest])
    through(ssem, R_RING, r2_in.at[pl.ds(1, ring - 1)])
    pair.wait_send()
    through(ssem, R_PLANE, r3_in.at[pl.ds(1, plane - 1)])
    line_loop(lines - zz, lambda copy: copy.wait_send())

    @pl.when(ends)
    def _():
        through(ssem, EDGE, sa_out.at[pl.ds(0, G), pl.ds(2 * SUB, SUB)])

    @pl.when(ctx < count - 1)
    def _():
        halo.wait_send()

    @pl.when(ctx > 0)
    def _():
        tail.wait_send()


def local(projected, short_filter, decay_rates, residues, output_grad, clip_bound):
    _, tokens, channels = projected.shape
    modes = decay_rates.shape[0]
    halves = channels // LANES
    block = tokens // SUB
    tp_size = lax.axis_size("tp")
    lines, planes = lax.axis_size("ctx") // G, tp_size // HI
    tile = pltpu.VMEM((SUB, LANES), F32)
    tiles = pltpu.VMEM((G, SUB, LANES), F32)
    edge = pltpu.VMEM((8, channels), F32)
    vmem = pl.BlockSpec(memory_space=pltpu.VMEM)
    return pl.pallas_call(
        functools.partial(kernel, modes, tp_size),
        out_shape=(
            jax.ShapeDtypeStruct((tokens, channels), jnp.bfloat16),
            jax.ShapeDtypeStruct((3, tokens, channels), jnp.bfloat16),
            jax.ShapeDtypeStruct(short_filter.shape, F32),
        ),
        in_specs=[pl.BlockSpec(memory_space=pltpu.HBM)] * 5 + [pl.BlockSpec(memory_space=pltpu.SMEM)],
        out_specs=(vmem, vmem, vmem),
        scratch_shapes=[
            pltpu.VMEM(projected.shape, projected.dtype),
            pltpu.VMEM(short_filter.shape, F32),
            pltpu.VMEM(decay_rates.shape, F32),
            pltpu.VMEM(residues.shape, F32),
            pltpu.VMEM(output_grad.shape, output_grad.dtype),
            pltpu.SemaphoreType.DMA((5,)),
            pltpu.VMEM((4 * halves, PAD + tokens, LANES), F32),
            pltpu.VMEM((4 * halves, block + 2, SUB, LANES), F32),
            pltpu.VMEM((3 * halves, block, SUB, LANES), F32),
            pltpu.VMEM((2 * halves, block, SUB, LANES), F32),
            pltpu.VMEM((2 * halves, block, SUB, LANES), F32),
            pltpu.VMEM((halves, modes, SUB, LANES), F32),
            pltpu.VMEM((halves, block, SUB, LANES), F32),
            pltpu.VMEM((2 * halves, modes, SUB, LANES), F32),
            pltpu.VMEM((G // 2, SUB, LANES), F32),
            pltpu.VMEM((G // 2, SUB, LANES), F32),
            pltpu.VMEM((halves, tokens, LANES), F32),
            pltpu.VMEM((3 * halves, tokens + 8, LANES), F32),
            edge, edge, tile, edge, edge,
            pltpu.VMEM((G, 3 * SUB, LANES), F32), pltpu.VMEM((G, 3 * SUB, LANES), F32), tiles,
            pltpu.VMEM((G, 6, SUB, LANES), F32), pltpu.VMEM((G, 6, SUB, LANES), F32),
            tile, tiles, tiles, tiles,
            tiles, tiles, pltpu.VMEM((ROWS, LANES), F32), pltpu.VMEM((HI * lines, ROWS, LANES), F32),
            pltpu.VMEM((CORES * ROWS, LANES), F32), pltpu.VMEM((G // CORES * planes, CORES * ROWS, LANES), F32),
            pltpu.SemaphoreType.DMA((11, 8)),
            pltpu.SemaphoreType.DMA((11, 8)),
        ],
        compiler_params=pltpu.CompilerParams(
            collective_id=0, has_side_effects=True, vmem_limit_bytes=32 * 1024 * 1024
        ),
    )(*(pltpu.with_memory_space_constraint(v, pltpu.HBM) for v in (projected, short_filter, decay_rates, residues, output_grad)), clip_bound)


def solution(mesh):
    placed = (
        P(None, "ctx", "tp"),
        P(None, None, "tp"),
        P(None, "tp"),
        P(None, "tp"),
        P("ctx", "tp"),
        P(),
    )
    return jax.shard_map(
        local,
        mesh=mesh,
        in_specs=placed,
        out_specs=(P("ctx", "tp"), P(None, "ctx", "tp"), P(None, None, "tp")),
        check_vma=False,
    )
```

```python
import functools

import jax
import jax.numpy as jnp
from jax import lax
from jax.experimental import pallas as pl
from jax.experimental.pallas import tpu as pltpu
from jax.sharding import PartitionSpec as P

MESH = pl.DeviceIdType.MESH
F32 = jnp.float32
LANES = 128
SUB = 8
PAD = 8
G = 8
HALO, EDGE, S_GROUP, S_LINE, S_BACK, W_GROUP, R_GROUP, R_RING, R_PAIR, R_PLANE, TAIL = range(11)
CORES = 2
ROWS = 4
HI = 2


def loop(start, stop, unroll, body, carry):
    def some(i, carry):
        for k in range(unroll):
            carry = body(start + i * unroll + k, carry)
        return carry

    return lax.fori_loop(0, (stop - start) // unroll, some, carry)


def kernel(
    modes, tp_size,
    proj_hbm, taps_hbm, rates_hbm, weights_hbm, cot_hbm, bound,
    gated, grads, filt,
    proj, taps, rates, weights, cot, in_sem,
    pf, ps, feat, xs, ys, lam, htab, excl, rown, wown, gat, fgs,
    halo_out, halo_in, edge_in, tail_out, tail_in,
    sa_out, sa_in, chunk, ga_out, ga_in, sb_out, sb_in, sc_out, sc_in,
    r1_out, r1_in, r2_out, r2_in, r3_out, r3_in,
    ssem, rsem,
):
    loads = [
        pltpu.make_async_copy(src, dst, in_sem.at[i])
        for i, (src, dst) in enumerate(
            ((proj_hbm, proj), (rates_hbm, rates), (taps_hbm, taps), (cot_hbm, cot), (weights_hbm, weights))
        )
    ]
    for load in loads:
        load.start()
    tokens = proj.shape[1]
    halves = proj.shape[2] // LANES
    block = tokens // SUB
    quarter = modes // (G // 2)
    ctx, tp = lax.axis_index("ctx"), lax.axis_index("tp")
    count = lax.axis_size("ctx")
    lines = count // G
    z, g = ctx // G, lax.rem(ctx, G)
    causal = g < G // 2
    zz = jnp.where(causal, z, lines - 1 - z)
    towards = jnp.where(causal, 1, -1)

    def at_group(d):
        return {"ctx": z * G + lax.rem(g + d, G), "tp": tp}

    x, hi = tp // HI, lax.rem(tp, HI)
    ring, planes = HI * lines, tp_size // HI
    zr = hi * lines + z

    def at_ring(d):
        there = lax.rem(zr + d, ring)
        return {"ctx": lax.rem(there, lines) * G + g, "tp": x * HI + there // lines}

    chips = G // CORES
    y, core = g // CORES, lax.rem(g, CORES)
    twin = 1 - core

    def at_plane(i):
        there = lax.rem(y + lax.rem(i, chips), chips) * CORES + core
        return {"ctx": z * G + there, "tp": lax.rem(x + i // chips, planes) * HI + hi}

    plane = planes * chips

    def at(c):
        return {"ctx": c, "tp": tp}

    halo_in[...] = jnp.zeros_like(halo_in)
    edge_in[...] = jnp.zeros_like(edge_in)
    tail_in[...] = jnp.zeros_like(tail_in)
    sb_in[...] = jnp.zeros_like(sb_in)

    barrier = pltpu.get_barrier_semaphore()
    def greet(first, last, dev):
        def signal(d, _):
            pl.semaphore_signal(barrier, inc=1, device_id=dev(d), device_id_type=MESH)

        lax.fori_loop(first, last, signal, None)

    greet(1, ring, at_ring)
    greet(1, G, at_group)
    greet(chips, plane, at_plane)
    ends, begins = jnp.logical_and(g == G - 1, z < lines - 1), z > 0

    @pl.when(ends)
    def _():
        greet(0, G - 1, lambda d: at(ctx + 1 + d))

    @pl.when(jnp.logical_and(begins, g < G - 1))
    def _():
        pl.semaphore_signal(barrier, inc=1, device_id=at(z * G - 1), device_id_type=MESH)

    def send(src, dst, step, d, dev):
        return pltpu.make_async_remote_copy(
            src_ref=src, dst_ref=dst, send_sem=ssem.at[step, d], recv_sem=rsem.at[step, d],
            device_id=dev, device_id_type=MESH,
        )

    def fan(order, src, dst, step, dev):
        for d in order:
            send(src(d), dst(d), step, 0, dev(d)).start()

    def far_first(n):
        return sorted(range(1, n), key=lambda d: -min(d, n - d))

    def through(sems, step, ref):
        pltpu.make_async_copy(ref, ref, sems.at[step, 0]).wait()

    def member_of(d):
        return lax.rem(g + d, G)

    rest = pl.ds(1, G - 1)
    tail_out[...] = jnp.zeros_like(tail_out)
    r1_out[...] = jnp.zeros_like(r1_out)
    ga_out[...] = jnp.zeros_like(ga_out)
    halo_out[...] = jnp.zeros_like(halo_out)
    for load in loads:
        load.wait()

    for h in range(halves):
        cols = slice(h * LANES, (h + 1) * LANES)
        for s in range(3):
            pf[s * halves + h, 0:PAD, :] = jnp.zeros((PAD, LANES), F32)
            pf[s * halves + h, PAD : PAD + tokens, :] = proj[s, :, cols].astype(F32)
        pf[3 * halves + h, PAD : PAD + tokens, :] = cot[:, cols].astype(F32)

    for m in range(modes):
        rate = rates[m : m + 1, :]
        keep = jnp.exp(-rate)
        for h in range(halves):
            lam[h, m] = jnp.broadcast_to(keep[:, h * LANES : (h + 1) * LANES], (SUB, LANES))
            row = h * quarter + m % quarter
            rown[m // quarter, row : row + 1, :] = rate[:, h * LANES : (h + 1) * LANES]
            wown[m // quarter, row : row + 1, :] = weights[m : m + 1, h * LANES : (h + 1) * LANES]

    def rows(b):
        return pl.ds(PAD + b, SUB, stride=block)

    def tap(s, j, h):
        return jnp.broadcast_to(taps[s, j : j + 1, h * LANES : (h + 1) * LANES], (SUB, LANES))

    def featurize(b, h):
        f = []
        for s in range(3):
            i = s * halves + h
            value = tap(s, 0, h) * ps[i, b + 2]
            value = value + tap(s, 1, h) * ps[i, b + 1]
            value = value + tap(s, 2, h) * ps[i, b]
            feat[i, b] = value
            f.append(value)
        xs[h, b] = f[1] * f[2]
        xs[halves + h, block - 1 - b] = ps[3 * halves + h, b + 2] * f[0]

    def turn(i, b):
        ps[i, b + 2] = pf[i, rows(b), :]

    for i in range(4 * halves):
        if i < 3 * halves:
            turn(i, -2)
            turn(i, -1)
        loop(0, block, 8, lambda b, _: turn(i, b), None)

    place = lax.broadcasted_iota(jnp.int32, (SUB, LANES), 0)
    inner = place >= 1
    for h in range(halves):
        loop(0, block, 4, lambda b, _: featurize(b, h), None)
        for b in range(2):
            xs[h, b] = jnp.where(inner, xs[h, b], 0.0)
            xs[halves + h, block - 1 - b] = jnp.where(inner, xs[halves + h, block - 1 - b], 0.0)

    for h in range(halves):
        cols = slice(h * LANES, (h + 1) * LANES)
        keeps = [lam[h, m] for m in range(modes)]

        def horner(b, state):
            front, back = xs[h, b], xs[halves + h, b]
            return tuple(
                state[2 * m + r] * keeps[m] + (front, back)[r] for m in range(modes) for r in range(2)
            )

        zero = jnp.zeros((SUB, LANES), F32)
        state = loop(0, block, 4, horner, (zero,) * (2 * modes))
        for m in range(modes):
            rate = rates[m : m + 1, cols]
            for r in range(2):
                value = state[2 * m + r]
                for k in (1, 2, 4):
                    fade = jnp.exp(-(block * k) * rate)
                    if r == 0:
                        value = value + jnp.where(place >= k, fade, 0.0) * pltpu.roll(value, k, 0)
                    else:
                        value = value + jnp.where(place < SUB - k, fade, 0.0) * pltpu.roll(value, SUB - k, 0)
                row = h * quarter + m % quarter
                owner = r * (G // 2) + m // quarter
                if r == 0:
                    excl[h, m] = jnp.where(place >= 1, pltpu.roll(value, 1, 0), 0.0)
                    sa_out[owner, row : row + 1, :] = value[SUB - 1 : SUB, :]
                else:
                    excl[halves + h, m] = jnp.where(place < SUB - 1, pltpu.roll(value, SUB - 1, 0), 0.0)
                    sa_out[owner, row : row + 1, :] = value[0:1, :]

    for h in range(halves):
        cols = slice(h * LANES, (h + 1) * LANES)

        def part(s, b):
            i = s * halves + h
            own = [taps[s, j : j + 1, cols] * pf[i, PAD + b - j : PAD + b - j + 1, :] for j in range(b + 1)]
            late = [
                taps[s, j : j + 1, cols] * pf[i, PAD + tokens + b - j : PAD + tokens + b - j + 1, :]
                for j in range(b + 1, 3)
            ]
            return sum(own[1:], own[0]), sum(late[1:], late[0])

        for s in range(3):
            halo_out[2 * s : 2 * s + 2, cols] = pf[s * halves + h, PAD + tokens - 2 : PAD + tokens, :]
        for b in range(2):
            q, k, v = (part(s, b) for s in range(3))
            other = pf[3 * halves + h, PAD + b : PAD + b + 1, :]
            none = jnp.zeros((1, LANES), F32)
            for owner in range(G):
                first, second = (k, v) if owner < G // 2 else ((other, none), q)
                for at_row, kind in ((SUB, 0), (2 * SUB, 1)):
                    row = at_row + b * halves + h
                    sa_out[owner, row : row + 1, :] = first[kind]
                    row = row + 2 * halves
                    sa_out[owner, row : row + 1, :] = second[kind]

    chain = modes // 2
    def grown(h, first):
        cols = slice(h * LANES, (h + 1) * LANES)
        keeps = [lam[h, m] for m in range(first, first + chain)]
        for s in range(3):
            def factor(b):
                return ps[3 * halves + h, b + 2] if s == 0 else feat[(3 - s) * halves + h, b]

            def grow(b, state, mask=None):
                b = block - 1 - b if s == 0 else b
                with_ = factor(b)
                if mask is not None:
                    with_ = jnp.where(mask, with_, 0.0)
                result = []
                for j in range(3):
                    u = with_ * ps[s * halves + h, b + 2 - j]
                    result += [state[j * chain + m] * keeps[m] + u for m in range(chain)]
                return tuple(result)

            state = (jnp.zeros((SUB, LANES), F32),) * (3 * chain)
            if s == 0:
                state = loop(0, block - 2, 2, grow, state)
                for b in range(block - 2, block):
                    state = grow(b, state, inner)
            else:
                for b in range(2):
                    state = grow(b, state, inner)
                state = loop(2, block, 2, grow, state)
            ahead = (place if s == 0 else SUB - 1 - place).astype(F32)
            for k in range(chain):
                m = first + k
                weight = jnp.exp(-(ahead * float(block) + 1.0) * rates[m : m + 1, cols]) * weights[m : m + 1, cols]
                owner = (0 if s == 0 else G // 2) + m // quarter
                row = h * quarter + m % quarter
                for j in range(3):
                    index = j if s == 0 else 3 * (s - 1) + j
                    ga_out[owner, index, row : row + 1, :] = jnp.sum(
                        state[j * chain + k] * weight, axis=0, keepdims=True
                    )

    pieces = [(h, first) for h in range(halves) for first in range(0, modes, chain)]
    for piece in pieces[:1]:
        grown(*piece)

    pl.semaphore_wait(
        barrier,
        (ring - 1) + (G - 1) + (plane - chips) + jnp.where(ends, G - 1, 0)
        + jnp.where(jnp.logical_and(begins, g < G - 1), 1, 0),
    )
    fan(far_first(G), lambda d: sa_out.at[member_of(d)], lambda d: sa_in.at[d], S_GROUP, at_group)
    @pl.when(ends)
    def _():
        fan(
            range(G), lambda d: sa_out.at[d, pl.ds(2 * SUB, SUB)], lambda d: edge_in, EDGE,
            lambda d: at((z + 1) * G + d),
        )

    halo = send(halo_out, halo_in, HALO, 0, at(ctx + 1))

    @pl.when(ctx < count - 1)
    def _():
        halo.start()

    sa_in[0] = sa_out[g]

    for piece in pieces[1:4 - 1]:
        grown(*piece)

    def both(row_of):
        return jnp.where(place < quarter, row_of(0), row_of(1))

    through(rsem, S_GROUP, sa_in.at[rest])

    @pl.when(begins)
    def _():
        through(rsem, EDGE, edge_in)

    own_rate = rown[lax.rem(g, G // 2)]
    fade = jnp.exp(-float(tokens) * own_rate)
    fade_group = jnp.exp(-float(tokens * G) * own_rate)

    def member(i):
        return jnp.where(causal, i, G - 1 - i)

    factors = (
        jnp.where(causal, jnp.exp(-float(tokens - 1) * own_rate), 1.0),
        jnp.where(causal, jnp.exp(-float(tokens - 2) * own_rate), jnp.exp(-own_rate)),
    )
    for i in range(G):
        of = lax.rem(g - i + G, G)
        before = edge_in[...] if i == 0 else sa_in[lax.rem(g - i + 1 + G, G), 2 * SUB : 3 * SUB, :]
        pair = sa_in[of, SUB : 2 * SUB, :] + before
        pair = pair[0 : 2 * halves, :] * pair[2 * halves : 4 * halves, :]
        value = sa_in[of, 0:SUB, :]
        for b in range(2):
            value = value + factors[b] * both(lambda h: pair[b * halves + h : b * halves + h + 1, :])
        chunk[i] = value

    value = jnp.zeros((SUB, LANES), F32)
    for i in range(G):
        value = value * fade + chunk[member(i)]
    sb_out[...] = value
    def along(d):
        return send(sb_out, sb_in.at[d], S_LINE, d, at((z + d * towards) * G + g))

    def line_loop(last, act):
        lax.fori_loop(1, last, lambda d, _: act(along(last - d)), None)

    line_loop(lines - zz, lambda copy: copy.start())
    for piece in pieces[4 - 1:]:
        grown(*piece)

    @pl.when(ctx > 0)
    def _():
        halo.wait_recv()

    for h in range(halves):
        for s in range(3):
            pf[s * halves + h, PAD - 2 : PAD, :] = halo_in[2 * s : 2 * s + 2, h * LANES : (h + 1) * LANES]
            turn(s * halves + h, -2)
            turn(s * halves + h, -1)
        for b in range(2):
            featurize(b, h)

    for q in range(G // 2):
        rate = rown[q]
        weight = wown[q]
        for s in range(3):
            for j in range(3):
                index = j if s == 0 else 3 * (s - 1) + j
                owner = (0 if s == 0 else G // 2) + q
                value = ga_out[owner, index]
                for b in range(2):
                    def product(h):
                        i = s * halves + h
                        if s == 0:
                            with_ = pf[3 * halves + h, PAD + b : PAD + b + 1, :]
                        else:
                            with_ = feat[(3 - s) * halves + h, b, 0:1, :]
                        return with_ * pf[i, PAD + b - j : PAD + b - j + 1, :]

                    power = float(b + 1 if s == 0 else tokens - b)
                    value = value + both(product) * (weight * jnp.exp(-power * rate))
                ga_out[owner, index] = value


    fan(far_first(G), lambda d: ga_out.at[member_of(d)], lambda d: ga_in.at[d], W_GROUP, at_group)
    ga_in[0] = ga_out[g]

    steps = lax.broadcasted_iota(jnp.int32, (block, LANES), 0).astype(F32)
    for h in range(halves):
        cols = slice(h * LANES, (h + 1) * LANES)
        total = jnp.zeros((block, LANES), F32)
        for m in range(modes):
            total = total + weights[m : m + 1, cols] * jnp.exp(-rates[m : m + 1, cols] * steps)
        for k in range(block):
            htab[h, k] = jnp.broadcast_to(total[k : k + 1, :], (SUB, LANES))

    def direct(hd, _):
        h = lax.rem(hd, halves)
        width = 8
        for b0 in range(0, block, width):
            acc = [None] * width
            for a0 in range(0, b0 + width, width):
                for a in range(a0, a0 + width):
                    x = xs[hd, a]
                    for i in range(width):
                        if b0 + i >= a:
                            term = htab[h, b0 + i - a] * x
                            acc[i] = term if acc[i] is None else acc[i] + term
            for i in range(width):
                ys[hd, b0 + i] = acc[i]

    lax.fori_loop(0, 2 * halves, direct, None)

    def readout(h, r, left):
        keeps = [lam[h, m] for m in range(modes)]

        def step(b, left):
            parts = list(left)
            while len(parts) > 1:
                parts = [parts[i] + parts[i + 1] for i in range(0, len(parts), 2)]
            ys[r * halves + h, b] = ys[r * halves + h, b] + parts[0]
            return tuple(left[m] * keeps[m] for m in range(modes))

        loop(0, block, 4, step, tuple(left))

    for h in range(halves):
        cols = slice(h * LANES, (h + 1) * LANES)
        for r in range(2):
            left = []
            for m in range(modes):
                value = excl[r * halves + h, m]
                if r == 0:
                    rate = rates[m : m + 1, cols]
                    behind = jnp.maximum(place - 1, 0).astype(F32) * float(block)
                    late = jnp.exp(-float(block - 1) * rate) * xs[h, 0, 0:1, :]
                    late = late + jnp.exp(-float(block - 2) * rate) * xs[h, 1, 0:1, :]
                    value = value + jnp.where(inner, jnp.exp(-behind * rate) * late, 0.0)
                left.append(value * (weights[m : m + 1, cols] * lam[h, m]))
            readout(h, r, left)

    def feature_grads(b, h):
        out, back = ys[h, b], ys[halves + h, block - 1 - b]
        return out, (
            ps[3 * halves + h, b + 2] * out,
            back * feat[2 * halves + h, b],
            back * feat[halves + h, b],
        )

    for h in range(halves):
        def gather(b, sums):
            _, fg = feature_grads(b, h)
            return tuple(
                sums[3 * s + j] + fg[s] * ps[s * halves + h, b + 2 - j] for s in range(3) for j in range(3)
            )

        sums = loop(0, block, 4, gather, (jnp.zeros((SUB, LANES), F32),) * 9)
        for e in range(9):
            unit = e * halves + h
            r1_out[unit // 3, unit % 3 : unit % 3 + 1, :] = jnp.sum(sums[e], axis=0, keepdims=True)

    line_loop(zz + 1, lambda copy: copy.wait_recv())
    value = jnp.zeros((SUB, LANES), F32)
    for d in range(lines - 1, 0, -1):
        value = value * fade_group + sb_in[d]
    for i in range(G):
        sc_out[member(i)] = value
        value = value * fade + chunk[member(i)]
    through(rsem, W_GROUP, ga_in.at[rest])

    for index in range(6):
        value = jnp.zeros((SUB, LANES), F32)
        for i in range(G):
            value = value + sc_out[i] * ga_in[lax.rem(g - i + G, G), index]
        for h in range(halves):
            total = jnp.sum(value[h * quarter : (h + 1) * quarter, :], axis=0, keepdims=True)
            for here, e in ((causal, index), (jnp.logical_not(causal), index + 3)):
                if e == index and index >= 3:
                    continue
                unit = e * halves + h
                row = unit % 3
                r1_out[unit // 3, row : row + 1, :] = r1_out[unit // 3, row : row + 1, :] + jnp.where(here, total, 0.0)
    fan(far_first(G), lambda d: r1_out.at[member_of(d)], lambda d: r1_in.at[d], R_GROUP, at_group)
    fan(far_first(G), lambda d: sc_out.at[member_of(d)], lambda d: sc_in.at[d], S_BACK, at_group)
    sc_in[0] = sc_out[g]
    r1_in[0] = r1_out[g]
    through(rsem, R_GROUP, r1_in.at[rest])
    value = r1_in[lax.rem(g + G, G)]
    for i in range(1, G):
        value = value + r1_in[lax.rem(g - i + G, G)]
    r2_out[...] = value[0:ROWS, :]
    r2_in[0] = value[0:ROWS, :]
    fan(far_first(ring), lambda d: r2_out, lambda d: r2_in.at[d], R_RING, at_ring)

    through(rsem, S_BACK, sc_in.at[rest])
    for h in range(halves):
        cols = slice(h * LANES, (h + 1) * LANES)
        for r in range(2):
            ahead = (place if r == 0 else SUB - 1 - place).astype(F32)
            left = []
            for m in range(modes):
                owner = r * (G // 2) + m // quarter
                row = h * quarter + m % quarter
                carry = sc_in[lax.rem(g - owner + G, G), row : row + 1, :]
                value = jnp.exp(-(float(block) * ahead + 1.0) * rates[m : m + 1, cols])
                left.append(value * (weights[m : m + 1, cols] * carry))
            readout(h, r, left)

    for h in range(halves):
        def finish(b, _):
            out, fg = feature_grads(b, h)
            gat[h, pl.ds(b, SUB, stride=block), :] = feat[h, b] * out
            for s in range(3):
                fgs[s * halves + h, pl.ds(b, SUB, stride=block), :] = fg[s]

        loop(0, block, 4, finish, None)
        for s in range(3):
            tail_out[2 * s : 2 * s + 2, h * LANES : (h + 1) * LANES] = fgs[s * halves + h, 0:2, :]
    tail = send(tail_out, tail_in, TAIL, 0, at(ctx - 1))

    @pl.when(ctx > 0)
    def _():
        tail.start()

    for h in range(halves):
        gated[:, h * LANES : (h + 1) * LANES] = gat[h].astype(gated.dtype)

    @pl.when(ctx < count - 1)
    def _():
        tail.wait_recv()

    for h in range(halves):
        for s in range(3):
            fgs[s * halves + h, tokens : tokens + 2, :] = tail_in[2 * s : 2 * s + 2, h * LANES : (h + 1) * LANES]
    for h in range(halves):
        cols = slice(h * LANES, (h + 1) * LANES)
        for s in range(3):
            i = s * halves + h
            back = taps[s, 0:1, cols] * fgs[i, 0:tokens, :]
            back = back + taps[s, 1:2, cols] * fgs[i, 1 : tokens + 1, :]
            back = back + taps[s, 2:3, cols] * fgs[i, 2 : tokens + 2, :]
            grads[s, :, cols] = back.astype(grads.dtype)

    through(rsem, R_RING, r2_in.at[pl.ds(1, ring - 1)])

    def whole(part):
        value = r2_in[lax.rem(zr - part * lines + ring, ring)]
        for i in range(1, lines):
            value = value + r2_in[lax.rem(zr - part * lines - i + ring, ring)]
        return value

    square = jnp.zeros((1, LANES), F32)
    for part in range(HI):
        value = whole(part)
        square = square + jnp.sum((value * value)[0 : ROWS - 1, :], axis=0, keepdims=True)
    for c in range(CORES):
        @pl.when(core == c)
        def _():
            r3_out[c * ROWS : (c + 1) * ROWS, :] = whole(hi)
            r3_out[(c + 1) * ROWS - 1 : (c + 1) * ROWS, :] = square

    pair = send(
        r3_out.at[pl.ds(core * ROWS, ROWS)], r3_out.at[pl.ds(core * ROWS, ROWS)], R_PAIR, 0, at(z * G + y * CORES + twin)
    )
    pair.start()
    through(rsem, R_PAIR, r3_out.at[pl.ds(twin * ROWS, ROWS)])
    r3_in[0] = r3_out[...]
    across = sorted(
        range(1, plane), key=lambda i: -(min(i % chips, chips - i % chips) + min(i // chips, planes - i // chips))
    )
    fan(across, lambda i: r3_out, lambda i: r3_in.at[i], R_PLANE, at_plane)
    through(rsem, R_PLANE, r3_in.at[pl.ds(1, plane - 1)])

    def from_plane(i, k):
        return r3_in[lax.rem(x - k + planes, planes) * chips + lax.rem(y - i + chips, chips)]

    pairs = [from_plane(i, x) for i in range(chips)]
    blocks = [pairs[i // CORES][i % CORES * ROWS : (i % CORES + 1) * ROWS, :] for i in range(G)]
    square = jnp.zeros((1, LANES), F32)
    for k in range(planes):
        for i in range(chips):
            both_cores = from_plane(i, k)
            for c in range(CORES):
                square = square + both_cores[(c + 1) * ROWS - 1 : (c + 1) * ROWS, :]
    norm = jnp.sqrt(jnp.sum(square, axis=1, keepdims=True))
    limit = bound[0]
    scale = limit / jnp.maximum(norm, limit)
    for s in range(3):
        for j in range(3):
            for h in range(halves):
                unit = (3 * s + j) * halves + h
                filt[s, j : j + 1, h * LANES : (h + 1) * LANES] = (
                    blocks[unit // 3][unit % 3 : unit % 3 + 1, :] * scale
                )

    for step, ref in (
        (S_GROUP, sa_in), (W_GROUP, ga_in), (S_BACK, sc_in), (R_GROUP, r1_in),
    ):
        through(ssem, step, ref.at[rest])
    through(ssem, R_RING, r2_in.at[pl.ds(1, ring - 1)])
    pair.wait_send()
    through(ssem, R_PLANE, r3_in.at[pl.ds(1, plane - 1)])
    line_loop(lines - zz, lambda copy: copy.wait_send())

    @pl.when(ends)
    def _():
        through(ssem, EDGE, sa_out.at[pl.ds(0, G), pl.ds(2 * SUB, SUB)])

    @pl.when(ctx < count - 1)
    def _():
        halo.wait_send()

    @pl.when(ctx > 0)
    def _():
        tail.wait_send()


def local(projected, short_filter, decay_rates, residues, output_grad, clip_bound):
    _, tokens, channels = projected.shape
    modes = decay_rates.shape[0]
    halves = channels // LANES
    block = tokens // SUB
    tp_size = lax.axis_size("tp")
    lines, planes = lax.axis_size("ctx") // G, tp_size // HI
    tile = pltpu.VMEM((SUB, LANES), F32)
    tiles = pltpu.VMEM((G, SUB, LANES), F32)
    edge = pltpu.VMEM((8, channels), F32)
    vmem = pl.BlockSpec(memory_space=pltpu.VMEM)
    return pl.pallas_call(
        functools.partial(kernel, modes, tp_size),
        out_shape=(
            jax.ShapeDtypeStruct((tokens, channels), jnp.bfloat16),
            jax.ShapeDtypeStruct((3, tokens, channels), jnp.bfloat16),
            jax.ShapeDtypeStruct(short_filter.shape, F32),
        ),
        in_specs=[pl.BlockSpec(memory_space=pltpu.HBM)] * 5 + [pl.BlockSpec(memory_space=pltpu.SMEM)],
        out_specs=(vmem, vmem, vmem),
        scratch_shapes=[
            pltpu.VMEM(projected.shape, projected.dtype),
            pltpu.VMEM(short_filter.shape, F32),
            pltpu.VMEM(decay_rates.shape, F32),
            pltpu.VMEM(residues.shape, F32),
            pltpu.VMEM(output_grad.shape, output_grad.dtype),
            pltpu.SemaphoreType.DMA((5,)),
            pltpu.VMEM((4 * halves, PAD + tokens, LANES), F32),
            pltpu.VMEM((4 * halves, block + 2, SUB, LANES), F32),
            pltpu.VMEM((3 * halves, block, SUB, LANES), F32),
            pltpu.VMEM((2 * halves, block, SUB, LANES), F32),
            pltpu.VMEM((2 * halves, block, SUB, LANES), F32),
            pltpu.VMEM((halves, modes, SUB, LANES), F32),
            pltpu.VMEM((halves, block, SUB, LANES), F32),
            pltpu.VMEM((2 * halves, modes, SUB, LANES), F32),
            pltpu.VMEM((G // 2, SUB, LANES), F32),
            pltpu.VMEM((G // 2, SUB, LANES), F32),
            pltpu.VMEM((halves, tokens, LANES), F32),
            pltpu.VMEM((3 * halves, tokens + 8, LANES), F32),
            edge, edge, tile, edge, edge,
            pltpu.VMEM((G, 3 * SUB, LANES), F32), pltpu.VMEM((G, 3 * SUB, LANES), F32), tiles,
            pltpu.VMEM((G, 6, SUB, LANES), F32), pltpu.VMEM((G, 6, SUB, LANES), F32),
            tile, tiles, tiles, tiles,
            pltpu.VMEM((G, ROWS, LANES), F32), pltpu.VMEM((G, ROWS, LANES), F32),
            pltpu.VMEM((ROWS, LANES), F32), pltpu.VMEM((HI * lines, ROWS, LANES), F32),
            pltpu.VMEM((CORES * ROWS, LANES), F32), pltpu.VMEM((G // CORES * planes, CORES * ROWS, LANES), F32),
            pltpu.SemaphoreType.DMA((11, 8)),
            pltpu.SemaphoreType.DMA((11, 8)),
        ],
        compiler_params=pltpu.CompilerParams(
            collective_id=0, has_side_effects=True, vmem_limit_bytes=32 * 1024 * 1024
        ),
    )(*(pltpu.with_memory_space_constraint(v, pltpu.HBM) for v in (projected, short_filter, decay_rates, residues, output_grad)), clip_bound)


def solution(mesh):
    placed = (
        P(None, "ctx", "tp"),
        P(None, None, "tp"),
        P(None, "tp"),
        P(None, "tp"),
        P("ctx", "tp"),
        P(),
    )
    return jax.shard_map(
        local,
        mesh=mesh,
        in_specs=placed,
        out_specs=(P("ctx", "tp"), P(None, "ctx", "tp"), P(None, None, "tp")),
        check_vma=False,
    )
```
